256 devices in a mesh: dp: 2 (over y_hi), tm: 32 (over z, y_lo, core), tensor: 4 (over x).
Axes of the slice: x: 4, y: 4 (y_hi: 2, y_lo: 2; y = y_hi * 2 + y_lo), z: 8, core: 2. Of those that a mesh axis runs over, the one named last changes fastest.
Arguments:
- queries: bfloat16 [2, 64, 256, 1280], P('dp', 'tm', None, 'tensor'), may hold values from -140 to 140
- key_vectors: bfloat16 [2, 64, 256, 1280], P('dp', 'tm', None, 'tensor'), may hold values from -4.1 to 4.1
- value_vectors: bfloat16 [2, 64, 256, 1280], P('dp', 'tm', None, 'tensor'), may hold values from -6 to 6
- normed: bfloat16 [2, 64, 256, 1280], P('dp', 'tm'), may hold values from -6 to 6
- grad_output: bfloat16 [2, 64, 256, 1280], P('dp', 'tm'), may hold values from -6 to 6
- w_qkv: bfloat16 [3, 1280, 1280], P(None, None, 'tensor'), may hold values from -0.15625 to 0.15625
- w_out: bfloat16 [1280, 1280], P('tensor'), may hold values from -0.15625 to 0.15625
Outputs:
- grad_normed: bfloat16 [2, 64, 256, 1280], P('dp', 'tm')
- grad_qkv: float32 [3, 1280, 1280], P(None, ('dp', 'tm'), 'tensor')
- grad_out: float32 [1280, 1280], P('tensor', ('dp', 'tm'))
The draws below stay inside these ranges and needn't reach their ends.
All inputs are finite; a program needn't handle non-finite values.
Results may differ from the reference program's by a relative error of at most 0.018.
Values may be sent and summed in bfloat16 or wider, within the bound.
No kernel may reach another device: no remote copies, remote signals or barrier semaphores. Data moves between devices by JAX's collectives and lax.ppermute only.
A program may use at most 128 MiB of HBM per device.

```python
import jax
import jax.numpy as jnp

D = 1280
HS = 80
PATCHES = 256
CLIPS = 2
FRAMES = 64
HD = 1280


def shared_keys(key):
    return jnp.clip(jax.random.normal(key, (CLIPS, FRAMES, PATCHES, HD), jnp.float32), -4.0, 4.0)


def draw_key_vectors(key, part):
    base = shared_keys(key)
    return base.astype(jnp.bfloat16)


def draw_queries(key, part):
    key = jax.random.fold_in(key, 7)
    own = jnp.clip(jax.random.normal(key, (CLIPS, FRAMES, PATCHES, HD), jnp.float32), -4.0, 4.0)
    return own.astype(jnp.bfloat16)


def spiked(result, stream_key, source, target, blocks, factor):
    def block_of(axis_at):
        return (jnp.arange(result.shape[axis_at]) // (result.shape[axis_at] // blocks)).reshape((-1,) + (1,) * (result.ndim - 1 - axis_at))

    one_side = jax.random.permutation(stream_key, blocks)[block_of(target)]
    second = (block_of(target) + blocks // 2) % blocks
    return jnp.where((block_of(source) == one_side) | (block_of(source) == second), factor * result, result)


def level_of(rng, dims, pieces, least, top_value):
    def one(axis_at, parts):
        heights = jax.random.uniform(jax.random.fold_in(jax.random.fold_in(rng, 6), axis_at), (parts,), jnp.float32, least / len(pieces), top_value / len(pieces))
        return jnp.repeat(jnp.exp(heights), dims[axis_at] // parts).reshape((-1,) + (1,) * (len(dims) - axis_at - 1))

    loudness = one(*pieces[0])
    for cut in pieces[1:]:
        loudness = loudness * one(*cut)
    return loudness


def bell_draw(stream_key, shape, deviation, bound, split=(), held_as=jnp.bfloat16):
    array = jax.random.normal(stream_key, shape, jnp.float32) * deviation
    if len(split) > 0:
        array = level_of(stream_key, shape, split, -0.22, 0.18) * array
    return jnp.clip(array, min=-bound, max=bound).astype(held_as)


def gaussian_with(key, dims, scale, limit, shards, heavy, held_as=jnp.bfloat16):
    drawn = scale * jax.random.normal(key, dims, jnp.float32)
    if shards:
        drawn = drawn * level_of(key, dims, shards, -0.22, 0.18)
    return jnp.clip(spiked(drawn, jax.random.fold_in(key, 3), *heavy), -limit, limit).astype(held_as)


def setup_inputs(seed: int = 0) -> dict:
    keys = jax.random.split(jax.random.key(seed), 8)
    return {
        "queries": draw_queries(jax.random.fold_in(keys[7], 71), 0),
        "key_vectors": draw_key_vectors(jax.random.fold_in(keys[7], 71), 0),
        "value_vectors": bell_draw(keys[2], (CLIPS, FRAMES, PATCHES, HD), 1.0, 6.0, ((0, 2), (1, 32), (3, 4))),
        "normed": gaussian_with(keys[3], (CLIPS, FRAMES, PATCHES, D), 1.0, 6.0, ((0, 2), (1, 32)), (1, 3, 32, 2.75)),
        "grad_output": gaussian_with(keys[4], (CLIPS, FRAMES, PATCHES, D), 1.0, 6.0, ((0, 2), (1, 32)), (1, 3, 32, 2.75)),
        "w_qkv": bell_draw(keys[5], (3, D, HD), D ** -0.5, 0.15625, ((2, 4),)),
        "w_out": bell_draw(keys[6], (HD, D), HD ** -0.5, 0.15625, ((0, 4),)),
    }


def attention_grads(queries, key_vectors, value_vectors, grad_attn):
    full_shape = queries.shape
    head_shape = full_shape[:3] + (full_shape[3] // HS, HS)
    query_heads = queries.reshape(head_shape).astype(jnp.float32)
    key_heads = key_vectors.reshape(head_shape).astype(jnp.float32)
    value_heads = value_vectors.reshape(head_shape).astype(jnp.float32)
    grad_heads = grad_attn.reshape(head_shape).astype(jnp.float32)
    temper = HS ** -0.5
    scores = jnp.einsum('cfphd,cgphd->cphfg', query_heads, key_heads) * temper
    probs = jax.nn.softmax(scores, axis=-1)
    weights = probs.astype(jnp.bfloat16).astype(jnp.float32)
    attended = jnp.einsum('cphfg,cgphd->cfphd', weights, value_heads).astype(jnp.bfloat16)
    grad_probs = jnp.einsum('cfphd,cgphd->cphfg', grad_heads, value_heads)
    row_delta = jnp.sum(probs * grad_probs, axis=-1, keepdims=True)
    grad_scores = (probs * (grad_probs - row_delta)).astype(jnp.bfloat16).astype(jnp.float32)
    grad_q = (jnp.einsum('cphfg,cgphd->cfphd', grad_scores, key_heads) * temper).astype(jnp.bfloat16)
    grad_k = (jnp.einsum('cphfg,cfphd->cgphd', grad_scores, query_heads) * temper).astype(jnp.bfloat16)
    grad_v = jnp.einsum('cphfg,cfphd->cgphd', weights, grad_heads).astype(jnp.bfloat16)
    return tuple(item.reshape(full_shape) for item in (attended, grad_q, grad_k, grad_v))


def reference(queries, key_vectors, value_vectors, normed, grad_output, w_qkv, w_out):
    rows_grad = grad_output.reshape(-1, D)
    grad_attn = jnp.dot(rows_grad, w_out.T, preferred_element_type=jnp.float32).astype(jnp.bfloat16)
    grad_attn = grad_attn.reshape(queries.shape)
    attended, grad_q, grad_k, grad_v = attention_grads(queries, key_vectors, value_vectors, grad_attn)
    grad_out = jnp.dot(attended.reshape(-1, HD).T, rows_grad, preferred_element_type=jnp.float32)
    rows_norm = normed.reshape(-1, D)
    grad_rows = [item.reshape(-1, HD) for item in (grad_q, grad_k, grad_v)]
    grad_qkv = jnp.stack([jnp.dot(rows_norm.T, item, preferred_element_type=jnp.float32) for item in grad_rows])
    total = jnp.zeros((rows_norm.shape[0], D), jnp.float32)
    for item, weight in zip(grad_rows, (w_qkv[0], w_qkv[1], w_qkv[2])):
        total = total + jnp.dot(item, weight.T, preferred_element_type=jnp.float32)
    grad_normed = total.astype(jnp.bfloat16).reshape(normed.shape)
    return grad_normed, grad_qkv, grad_out
```

```python
import functools

import jax
import jax.numpy as jnp
import numpy as np
from jax import lax
from jax.experimental import pallas as pl
from jax.experimental.pallas import tpu as pltpu
from jax.sharding import Mesh
from jax.sharding import PartitionSpec as P

HS = 80
HEADS = 4
W = HEADS * HS
D = 1280
NX = 4
NT = 32
FR = 2
PT = 8
TOK = 512
TEMPER = HS ** (-0.5)
TM = ("z", "yl", "core")
Y = ("dp", "yl")
BF = jnp.bfloat16
F32 = jnp.float32
LIMIT = 48 * 1024 * 1024


def feature_order():
    order = np.zeros(D, np.int32)
    at = 0
    for core in range(2):
        for y in range(4):
            for z in range(8):
                dp, yl = divmod(y, 2)
                start = (((dp * 8 + z) * 2 + yl) * 2 + core) * 20
                order[at : at + 20] = np.arange(start, start + 20)
                at += 20
    return order.reshape(NX, 1, W)


def dot(a, b):
    return lax.dot_general(a, b, (((1,), (0,)), ((), ())), preferred_element_type=F32)


def dot_nt(a, b):
    return lax.dot_general(a, b, (((1,), (1,)), ((), ())), preferred_element_type=F32)


def call(kernel, out_shape, flops=0, grid_spec=None, **kw):
    params = pltpu.CompilerParams(vmem_limit_bytes=LIMIT)
    cost = pl.CostEstimate(flops=flops, bytes_accessed=4_000_000, transcendentals=0)
    if grid_spec is not None:
        kw["grid_spec"] = grid_spec
    return pl.pallas_call(kernel, out_shape=out_shape, compiler_params=params, cost_estimate=cost, **kw)


def to_chunks(rows):
    width = rows.shape[-1]
    low = rows[: TOK // 2].reshape(NT, PT, width)
    high = rows[TOK // 2 :].reshape(NT, PT, width)
    return jnp.concatenate([low, high], axis=1).astype(BF)


def one_hot(feat_ref):
    places = lax.broadcasted_iota(jnp.int32, (D, W), 0)
    return jnp.where(places == feat_ref[...], 1.0, 0.0).astype(BF)


def pick_kernel(feat_ref, n_ref, go_ref, out_ref):
    pick = one_hot(feat_ref)
    for at, ref in enumerate((n_ref, go_ref)):
        rows = dot(ref[...].reshape(TOK, D), pick)
        out_ref[:, :, at * W : (at + 1) * W] = to_chunks(rows)


def pack_kernel(q_ref, k_ref, v_ref, out_ref):
    for at, ref in enumerate((q_ref, k_ref, v_ref)):
        rows = ref[...].astype(F32).reshape(TOK, W)
        out_ref[:, :, at * W : (at + 1) * W] = to_chunks(rows)


def reorder_kernel(feat_ref, w_ref, out_ref):
    for at in range(NX):
        out_ref[at] = dot(w_ref[...], one_hot(feat_ref.at[at])).astype(BF)


def attend_kernel(qkv_ref, ngo_ref, wout_ref, wqkv_ref, grads_ref, gnp_ref, g_s, kt_s, vt_s):
    acc = jnp.zeros((TOK, W), F32)
    for at in range(NX):
        acc = acc + dot_nt(ngo_ref[at].reshape(TOK, 2 * W)[:, W:], wout_ref[at])
    ga = acc.astype(BF)
    qkv = qkv_ref[...].reshape(TOK, 3 * W)
    q, k, v = qkv[:, :W], qkv[:, W : 2 * W], qkv[:, 2 * W :]
    q_t = q.astype(F32).T.astype(BF)
    ga_t = ga.astype(F32).T.astype(BF)
    block = 256
    row_patch = lax.broadcasted_iota(jnp.int32, (block, TOK), 0) % PT
    col_patch = lax.broadcasted_iota(jnp.int32, (block, TOK), 1) % PT
    same = row_patch == col_patch
    for h in range(HEADS):
        cols = slice(h * HS, (h + 1) * HS)
        kh, vh = k[:, cols], v[:, cols]
        dk_t = dv_t = None
        for b in range(TOK // block):
            rows = slice(b * block, (b + 1) * block)
            scores = dot_nt(q[rows, cols], kh) * TEMPER
            scores = jnp.where(same, scores, -jnp.inf)
            top = jnp.max(scores, axis=1, keepdims=True)
            powers = jnp.exp(scores - top)
            probs = powers / jnp.sum(powers, axis=1, keepdims=True)
            weights = probs.astype(BF)
            g_s[rows, 3 * W + h * HS : 3 * W + (h + 1) * HS] = dot(weights, vh)
            grad_probs = dot_nt(ga[rows, cols], vh)
            delta = jnp.sum(probs * grad_probs, axis=1, keepdims=True)
            grad_scores = (probs * (grad_probs - delta)).astype(BF)
            g_s[rows, h * HS : (h + 1) * HS] = dot(grad_scores, kh) * TEMPER
            dk_part = dot(q_t[cols, rows], grad_scores)
            dv_part = dot(ga_t[cols, rows], weights)
            dk_t = dk_part if dk_t is None else dk_t + dk_part
            dv_t = dv_part if dv_t is None else dv_t + dv_part
        kt_s[cols, :] = dk_t * TEMPER
        vt_s[cols, :] = dv_t
    g_s[:, W : 2 * W] = kt_s[...].T
    g_s[:, 2 * W : 3 * W] = vt_s[...].T
    grads = g_s[...].astype(BF)
    grads_ref[...] = grads
    for at in range(NX):
        part = jnp.zeros((TOK, W), F32)
        for i in range(3):
            part = part + dot_nt(grads[:, i * W : (i + 1) * W], wqkv_ref[i, at * W : (at + 1) * W, :])
        gnp_ref[at] = part.astype(BF)


def weight_kernel(half_ref, ngo_ref, grads_ref, out_ref):
    del half_ref
    ngo_t = ngo_ref[0].reshape(TOK, 2 * W).astype(F32).T.astype(BF)
    out_ref[:, : 3 * W] = dot(ngo_t[:W], grads_ref[:, : 3 * W]).astype(out_ref.dtype)
    out_ref[:, 3 * W :] = dot(ngo_t[W:], grads_ref[:, 3 * W :]).astype(out_ref.dtype)


def weight_half(half, ngo, grads, dtype):
    spec = pltpu.PrefetchScalarGridSpec(
        num_scalar_prefetch=1,
        grid=(2,),
        in_specs=[
            pl.BlockSpec((1, NT, 2 * PT, 2 * W), lambda j, half: (half[0] * 2 + j, 0, 0, 0)),
            pl.BlockSpec((TOK, 4 * W), lambda j, half: (0, 0)),
        ],
        out_specs=pl.BlockSpec((W, 4 * W), lambda j, half: (j, 0)),
    )
    return call(weight_kernel, jax.ShapeDtypeStruct((2 * W, 4 * W), dtype), 850_000_000, spec)(half, ngo, grads)


def spread_kernel(in_ref, out_ref):
    for at in range(NX):
        block = in_ref[at].astype(F32)
        for f in range(FR):
            rows = block[:, f * PT : (f + 1) * PT, :].reshape(NT * PT, W)
            out_ref[f, :, at * W : (at + 1) * W] = rows.astype(BF)


def on_device(queries, key_vectors, value_vectors, normed, grad_output, w_qkv, w_out):
    order = jnp.asarray(feature_order())
    x = lax.axis_index("x")
    core = lax.axis_index("core")
    mine = lax.dynamic_index_in_dim(order, x, 0, keepdims=False)
    ngo = call(pick_kernel, jax.ShapeDtypeStruct((NT, 2 * PT, 2 * W), BF), 850_000_000)(
        mine, normed[0], grad_output[0]
    )
    ngo = lax.all_to_all(ngo, TM, 0, 0, tiled=True)
    ngo = lax.all_gather(ngo, "x", axis=0)
    qkv = call(pack_kernel, jax.ShapeDtypeStruct((NT, 2 * PT, 3 * W), BF))(
        queries[0], key_vectors[0], value_vectors[0]
    )
    qkv = lax.all_to_all(qkv, TM, 0, 0, tiled=True)
    w_ordered = call(reorder_kernel, jax.ShapeDtypeStruct((NX, W, W), BF), 1_000_000_000)(order, w_out)
    grads, part_norm = call(
        attend_kernel,
        (jax.ShapeDtypeStruct((TOK, 4 * W), BF), jax.ShapeDtypeStruct((NX, TOK, W), BF)),
        5_000_000_000,
        scratch_shapes=[pltpu.VMEM((TOK, 4 * W), F32), pltpu.VMEM((W, TOK), F32), pltpu.VMEM((W, TOK), F32)],
    )(qkv, ngo, w_ordered, w_qkv)

    sent = weight_half((1 - core).reshape(1), ngo, grads, BF)
    got = lax.ppermute(sent, "core", [(0, 1), (1, 0)])
    kept = weight_half(core.reshape(1), ngo, grads, F32)
    both = (kept + got.astype(F32)).astype(BF).reshape(4, D // 8, 4 * W)
    quarter = lax.psum_scatter(both, Y, scatter_dimension=0, tiled=True)

    part_norm = lax.all_to_all(part_norm, "x", 0, 0, tiled=True)
    own_norm = jnp.sum(part_norm.astype(F32), axis=0).astype(BF).reshape(NT, 2 * PT, W)
    own_norm = lax.all_to_all(own_norm, TM, 0, 0, tiled=True)
    all_norm = lax.all_gather(own_norm, "x", axis=0)
    grad_normed = call(spread_kernel, jax.ShapeDtypeStruct((FR, 256, D), BF))(all_norm)

    pieces = lax.all_to_all(quarter.reshape(8, 20, 4 * W), "z", 0, 0, tiled=True)
    total = jnp.sum(pieces.astype(F32), axis=0)
    grad_qkv = total[:, : 3 * W].reshape(20, 3, W).transpose(1, 0, 2)
    grad_out = total[:, 3 * W :].T
    return (grad_normed[None], grad_qkv, grad_out)


def solution(mesh):
    own = Mesh(mesh.devices.reshape(2, 8, 2, 2, 4), ("dp", "z", "yl", "core", "x"))
    in_specs = (
        P("dp", TM, None, "x"),
        P("dp", TM, None, "x"),
        P("dp", TM, None, "x"),
        P("dp", TM, None, None),
        P("dp", TM, None, None),
        P(None, None, "x"),
        P("x", None),
    )
    out_specs = (
        P("dp", TM, None, None),
        P(None, ("dp",) + TM, "x"),
        P("x", ("dp",) + TM),
    )
    return jax.shard_map(on_device, mesh=own, in_specs=in_specs, out_specs=out_specs, check_vma=False)
```

```python
import functools

import jax
import jax.numpy as jnp
import numpy as np
from jax import lax
from jax.experimental import pallas as pl
from jax.experimental.pallas import tpu as pltpu
from jax.sharding import Mesh
from jax.sharding import PartitionSpec as P

HS = 80
HEADS = 4
W = HEADS * HS
D = 1280
NX = 4
NT = 32
FR = 2
PT = 8
TOK = 512
FRAMES = 64
LANES = 128
TILES = 4 * W // LANES
BLOCK = 128
TEMPER = HS ** (-0.5)
TM = ("z", "yl", "core")
Y = ("dp", "yl")
BF = jnp.bfloat16
F32 = jnp.float32
LIMIT = 48 * 1024 * 1024


def feature_order():
    order = np.zeros(D, np.int32)
    at = 0
    for core in range(2):
        for y in range(4):
            for z in range(8):
                dp, yl = divmod(y, 2)
                start = (((dp * 8 + z) * 2 + yl) * 2 + core) * 20
                order[at : at + 20] = np.arange(start, start + 20)
                at += 20
    return order.reshape(NX, 1, W)


def dot(a, b):
    return lax.dot_general(a, b, (((1,), (0,)), ((), ())), preferred_element_type=F32)


def dot_nt(a, b):
    return lax.dot_general(a, b, (((1,), (1,)), ((), ())), preferred_element_type=F32)


def call(kernel, out_shape, flops=0, grid_spec=None, limit=LIMIT, **kw):
    params = pltpu.CompilerParams(vmem_limit_bytes=limit)
    cost = pl.CostEstimate(flops=flops, bytes_accessed=4_000_000, transcendentals=0)
    if grid_spec is not None:
        kw["grid_spec"] = grid_spec
    return pl.pallas_call(kernel, out_shape=out_shape, compiler_params=params, cost_estimate=cost, **kw)


def to_chunks(rows):
    width = rows.shape[-1]
    low = rows[: TOK // 2].reshape(NT, PT, width)
    high = rows[TOK // 2 :].reshape(NT, PT, width)
    return jnp.concatenate([low, high], axis=1).astype(BF)


def one_hot(feat_ref):
    places = lax.broadcasted_iota(jnp.int32, (D, W), 0)
    return jnp.where(places == feat_ref[...], 1.0, 0.0).astype(BF)


def prepare_kernel(feat_ref, n_ref, go_ref, q_ref, k_ref, v_ref, ngo_ref, qkv_ref):
    pick = one_hot(feat_ref)
    for at, ref in enumerate((n_ref, go_ref)):
        rows = dot(ref[...].reshape(TOK, D), pick)
        ngo_ref[:, :, at * W : (at + 1) * W] = to_chunks(rows)
    for at, ref in enumerate((q_ref, k_ref, v_ref)):
        rows = jnp.concatenate([ref[f].astype(F32).T for f in range(FR)], axis=0)
        qkv_ref[:, :, at * W : (at + 1) * W] = to_chunks(rows)


def reorder_kernel(feat_ref, w_ref, out_ref):
    for at in range(NX):
        out_ref[at] = dot(w_ref[...], one_hot(feat_ref.at[at])).astype(BF)


def attend_kernel(x_ref, qkv_ref, ngo_ref, wout_ref, wqkv_ref, grads_ref, *rest):
    norm_refs, (wide_s, rows_s, all_t, g_t, norm_s) = rest[:NX], rest[NX:]
    acc = jnp.zeros((TOK, W), F32)
    for at in range(NX):
        acc = acc + dot_nt(ngo_ref[at].reshape(TOK, 2 * W)[:, W:], wout_ref[at])
    ga = acc.astype(BF).astype(F32)
    half = LANES // 2
    for t in range(7):
        wide_s[t] = qkv_ref[:, :, t * LANES : (t + 1) * LANES].reshape(TOK, LANES).astype(F32)
    wide_s[7, :, :half] = qkv_ref[:, :, 7 * LANES :].reshape(TOK, half).astype(F32)
    wide_s[7, :, half:] = ga[:, :half]
    for t in (8, 9):
        wide_s[t] = ga[:, (t - 8) * LANES + half : (t - 7) * LANES + half]
    for p in range(PT):
        for t in range(TILES):
            rows_s[p * FRAMES : (p + 1) * FRAMES, t * LANES : (t + 1) * LANES] = wide_s[
                t, pl.ds(p, FRAMES, stride=PT), :
            ].astype(BF)
    all_t[...] = rows_s[...].T
    row_patch = lax.broadcasted_iota(jnp.int32, (BLOCK, BLOCK), 0) // FRAMES
    col_patch = lax.broadcasted_iota(jnp.int32, (BLOCK, BLOCK), 1) // FRAMES
    same = row_patch == col_patch
    for b in range(TOK // BLOCK):
        rows = slice(b * BLOCK, (b + 1) * BLOCK)
        for h in range(HEADS):
            at = [slice(i * W + h * HS, i * W + (h + 1) * HS) for i in range(4)]
            q_t, k_t, v_t, ga_t = [all_t[cols, rows] for cols in at]
            scores = dot(rows_s[rows, at[1]], q_t) * TEMPER
            scores = jnp.where(same, scores, -jnp.inf)
            powers = jnp.exp(scores - jnp.max(scores, axis=0, keepdims=True))
            probs = powers * (1.0 / jnp.sum(powers, axis=0, keepdims=True))
            weights = probs.astype(BF)
            g_t[at[3], rows] = dot(v_t, weights)
            grad_probs = dot(rows_s[rows, at[2]], ga_t)
            delta = jnp.sum(probs * grad_probs, axis=0, keepdims=True)
            grad_scores = (probs * (grad_probs - delta)).astype(BF)
            g_t[at[0], rows] = dot(k_t, grad_scores) * TEMPER
            g_t[at[1], rows] = dot_nt(q_t, grad_scores) * TEMPER
            g_t[at[2], rows] = dot_nt(ga_t, weights)
    for t in range(TILES):
        tile = g_t[t * LANES : (t + 1) * LANES, :].T
        for p in range(PT):
            wide_s[t, pl.ds(p, FRAMES, stride=PT), :] = tile[p * FRAMES : (p + 1) * FRAMES]
    for t in range(TILES):
        grads_ref[:, t * LANES : (t + 1) * LANES] = wide_s[t].astype(BF)
    norm = dot(grads_ref[:, : 3 * W], wqkv_ref[...])
    for at in range(NX):
        part = norm[:, at * W : (at + 1) * W].reshape(NT, 2 * PT, W)
        slot = lax.rem(at + NX - x_ref[0], NX)
        for f in range(FR):
            norm_s[slot, :, f * W : (f + 1) * W] = part[:, f * PT : (f + 1) * PT, :].reshape(NT * PT, W).astype(BF)
    for at in range(NX):
        norm_refs[at][...] = norm_s[at]


def attend(x, qkv, ngo, w_ordered, w_qkv):
    scalar = pl.BlockSpec(memory_space=pltpu.SMEM)
    whole = pl.BlockSpec(memory_space=pltpu.VMEM)
    return call(
        attend_kernel,
        (jax.ShapeDtypeStruct((TOK, 4 * W), BF),) + (jax.ShapeDtypeStruct((TOK // 2, 2 * W), BF),) * NX,
        5_000_000_000,
        in_specs=[scalar] + [whole] * 4,
        scratch_shapes=[
            pltpu.VMEM((TILES, TOK, LANES), F32),
            pltpu.VMEM((TOK, 4 * W), BF),
            pltpu.VMEM((4 * W, TOK), BF),
            pltpu.VMEM((4 * W, TOK), F32),
            pltpu.VMEM((NX, TOK // 2, 2 * W), BF),
        ],
    )(x, qkv, ngo, w_ordered, w_qkv)


def weight_kernel(half_ref, ngo_ref, grads_ref, *refs):
    del half_ref
    out_ref = refs[-1]
    ngo_t = ngo_ref[0].reshape(TOK, 2 * W).astype(F32).T.astype(BF)
    for rows, cols in ((slice(0, W), slice(0, 3 * W)), (slice(W, 2 * W), slice(3 * W, 4 * W))):
        total = dot(ngo_t[rows], grads_ref[:, cols])
        if len(refs) == 2:
            total = total + refs[0][:, cols].astype(F32)
        out_ref[:, cols] = total.astype(BF)


def weight_half(half, ngo, grads, *got):
    block = pl.BlockSpec((W, 4 * W), lambda j, half: (j, 0))
    spec = pltpu.PrefetchScalarGridSpec(
        num_scalar_prefetch=1,
        grid=(2,),
        in_specs=[
            pl.BlockSpec((1, NT, 2 * PT, 2 * W), lambda j, half: (half[0] * 2 + j, 0, 0, 0)),
            pl.BlockSpec((TOK, 4 * W), lambda j, half: (0, 0)),
        ]
        + [block] * len(got),
        out_specs=block,
    )
    shape = jax.ShapeDtypeStruct((2 * W, 4 * W), BF)
    return call(weight_kernel, shape, 4_000_000_000, spec)(half, ngo, grads, *got)


def add_kernel(*refs):
    total = refs[0][...].astype(F32)
    for ref in refs[1:-1]:
        total = total + ref[...].astype(F32)
    refs[-1][...] = total.astype(BF)


def spread_kernel(x_ref, *refs):
    out_ref = refs[-1]
    for at in range(NX):
        for k in range(NX):

            @pl.when(lax.rem(x_ref[0] + NX - k, NX) == at)
            def _(at=at, k=k):
                for f in range(FR):
                    out_ref[f, :, at * W : (at + 1) * W] = refs[k][:, f * W : (f + 1) * W]


def shift(array, k):
    return lax.ppermute(array, "x", [(i, (i + k) % NX) for i in range(NX)])


def on_device(queries, key_vectors, value_vectors, normed, grad_output, w_qkv, w_out):
    order = jnp.asarray(feature_order())
    x = lax.axis_index("x")
    core = lax.axis_index("core")
    scalar = pl.BlockSpec(memory_space=pltpu.SMEM)
    whole = pl.BlockSpec(memory_space=pltpu.VMEM)
    mine = lax.dynamic_index_in_dim(order, x, 0, keepdims=False)
    ngo, qkv = call(
        prepare_kernel,
        (jax.ShapeDtypeStruct((NT, 2 * PT, 2 * W), BF), jax.ShapeDtypeStruct((NT, 2 * PT, 3 * W), BF)),
        850_000_000,
        limit=60 * 1024 * 1024,
    )(mine, normed[0], grad_output[0], *[jnp.swapaxes(item[0], 1, 2) for item in (queries, key_vectors, value_vectors)])
    ngo = lax.all_to_all(ngo, TM, 0, 0, tiled=True)
    ngo = lax.all_gather(ngo, "x", axis=0)
    qkv = lax.all_to_all(qkv, TM, 0, 0, tiled=True)
    w_ordered = call(reorder_kernel, jax.ShapeDtypeStruct((NX, W, W), BF), 1_000_000_000)(order, w_out)
    grads, *parts = attend(x.reshape(1), qkv, ngo, w_ordered, jnp.swapaxes(w_qkv, 1, 2).reshape(3 * W, D))

    moved = [parts[0]] + [shift(parts[k], k) for k in range(1, NX)]
    sent = weight_half((1 - core).reshape(1), ngo, grads)
    got = lax.ppermute(sent, "core", [(0, 1), (1, 0)])
    both = weight_half(core.reshape(1), ngo, grads, got).reshape(4, D // 8, 4 * W)
    quarter = lax.psum_scatter(both, Y, scatter_dimension=0, tiled=True)

    own_norm = call(add_kernel, jax.ShapeDtypeStruct((TOK // 2, 2 * W), BF), 40_000_000_000)(*moved)
    own_norm = lax.all_to_all(own_norm.reshape(NT, PT, 2 * W), TM, 0, 0, tiled=True).reshape(TOK // 2, 2 * W)
    all_norm = [own_norm] + [shift(own_norm, k) for k in range(1, NX)]
    grad_normed = call(
        spread_kernel, jax.ShapeDtypeStruct((FR, TOK // 2, D), BF), in_specs=[scalar] + [whole] * NX
    )(x.reshape(1), *all_norm)

    pieces = lax.all_to_all(quarter.reshape(8, 20, 4 * W), "z", 0, 0, tiled=True)
    total = jnp.sum(pieces.astype(F32), axis=0)
    grad_qkv = total[:, : 3 * W].reshape(20, 3, W).transpose(1, 0, 2)
    grad_out = total[:, 3 * W :].T
    return (grad_normed[None], grad_qkv, grad_out)


def solution(mesh):
    own = Mesh(mesh.devices.reshape(2, 8, 2, 2, 4), ("dp", "z", "yl", "core", "x"))
    in_specs = (
        P("dp", TM, None, "x"),
        P("dp", TM, None, "x"),
        P("dp", TM, None, "x"),
        P("dp", TM, None, None),
        P("dp", TM, None, None),
        P(None, None, "x"),
        P("x", None),
    )
    out_specs = (
        P("dp", TM, None, None),
        P(None, ("dp",) + TM, "x"),
        P("x", ("dp",) + TM),
    )
    return jax.shard_map(on_device, mesh=own, in_specs=in_specs, out_specs=out_specs, check_vma=False)
```

```python
import functools

import jax
import jax.numpy as jnp
import numpy as np
from jax import lax
from jax.experimental import pallas as pl
from jax.experimental.pallas import tpu as pltpu
from jax.sharding import Mesh
from jax.sharding import PartitionSpec as P

HS = 80
HEADS = 4
W = HEADS * HS
D = 1280
NX = 4
NT = 32
FR = 2
PT = 8
TOK = 512
FRAMES = 64
LANES = 128
GO = 384
TILES = 4 * W // LANES
BLOCK = 128
TEMPER = HS ** (-0.5)
TM = ("z", "yl", "core")
Y = ("dp", "yl")
BF = jnp.bfloat16
F32 = jnp.float32
LIMIT = 48 * 1024 * 1024


def feature_order():
    order = np.zeros(D, np.int32)
    at = 0
    for core in range(2):
        for y in range(4):
            for z in range(8):
                dp, yl = divmod(y, 2)
                start = (((dp * 8 + z) * 2 + yl) * 2 + core) * 20
                order[at : at + 20] = np.arange(start, start + 20)
                at += 20
    return order.reshape(NX, 1, W)


def dot(a, b):
    return lax.dot_general(a, b, (((1,), (0,)), ((), ())), preferred_element_type=F32)


def dot_nt(a, b):
    return lax.dot_general(a, b, (((1,), (1,)), ((), ())), preferred_element_type=F32)


def call(kernel, out_shape, flops=0, grid_spec=None, limit=LIMIT, **kw):
    params = pltpu.CompilerParams(vmem_limit_bytes=limit)
    cost = pl.CostEstimate(flops=flops, bytes_accessed=4_000_000, transcendentals=0)
    if grid_spec is not None:
        kw["grid_spec"] = grid_spec
    return pl.pallas_call(kernel, out_shape=out_shape, compiler_params=params, cost_estimate=cost, **kw)


def to_chunks(rows):
    width = rows.shape[-1]
    half = rows.shape[0] // 2
    low = rows[:half].reshape(-1, PT, width)
    high = rows[half:].reshape(-1, PT, width)
    return jnp.concatenate([low, high], axis=1).astype(BF)


def one_hot(feat):
    places = lax.broadcasted_iota(jnp.int32, (D, W), 0)
    return jnp.where(places == feat, 1.0, 0.0).astype(BF)


def pick_kernel(x_ref, order_ref, go_ref, n_ref, out_ref, pick_s):
    @pl.when(pl.program_id(0) == 0)
    def _():
        pick_s[...] = one_hot(order_ref[x_ref[0]])

    for at, ref in enumerate((go_ref, n_ref)):
        rows = dot(ref[...].reshape(-1, D), pick_s[...])
        out_ref[:, :, at * W : (at + 1) * W] = to_chunks(rows)


def pick(x, order, grad_output, normed):
    steps = 4
    block = pl.BlockSpec((FR, NT * PT // steps, D), lambda i: (0, i, 0))
    return call(
        pick_kernel,
        jax.ShapeDtypeStruct((NT, 2 * PT, 2 * W), BF),
        850_000_000,
        limit=60 * 1024 * 1024,
        grid=(steps,),
        in_specs=[
            pl.BlockSpec(memory_space=pltpu.SMEM),
            pl.BlockSpec((NX, 1, W), lambda i: (0, 0, 0)),
            block,
            block,
        ],
        out_specs=pl.BlockSpec((NT // steps, 2 * PT, 2 * W), lambda i: (i, 0, 0)),
        scratch_shapes=[pltpu.VMEM((D, W), BF)],
    )(x, order, grad_output, normed)


def pack_kernel(q_ref, k_ref, v_ref, qkv_ref):
    for at, ref in enumerate((q_ref, k_ref, v_ref)):
        rows = jnp.concatenate([ref[f].astype(F32).T for f in range(FR)], axis=0)
        qkv_ref[:, :, at * W : (at + 1) * W] = to_chunks(rows)


def reorder_kernel(feat_ref, w_ref, out_ref):
    for at in range(NX):
        out_ref[at] = dot(w_ref[...], one_hot(feat_ref[at])).astype(BF)


def attend_kernel(x_ref, qkv_ref, gon_ref, wout_ref, wqkv_hbm, grads_ref, *rest):
    norm_refs, (wide_s, rows_s, all_t, g_t, norm_s, go_s, wqkv_s, sems) = rest[:NX], rest[NX:]
    copies = [
        pltpu.make_async_copy(gon_ref.at[at, :, :, pl.ds(0, GO)], go_s.at[at], sems.at[at]) for at in range(NX)
    ]
    copies.append(pltpu.make_async_copy(wqkv_hbm, wqkv_s, sems.at[NX]))
    for copy in copies:
        copy.start()
    half = LANES // 2
    for t in range(7):
        wide_s[t] = qkv_ref[:, :, t * LANES : (t + 1) * LANES].reshape(TOK, LANES).astype(F32)
    wide_s[7, :, :half] = qkv_ref[:, :, 7 * LANES :].reshape(TOK, half).astype(F32)
    acc = jnp.zeros((TOK, W), F32)
    for at in range(NX):
        copies[at].wait()
        acc = acc + dot_nt(go_s[at].reshape(TOK, GO)[:, :W], wout_ref[at])
    ga = acc.astype(BF).astype(F32)
    wide_s[7, :, half:] = ga[:, :half]
    for t in (8, 9):
        wide_s[t] = ga[:, (t - 8) * LANES + half : (t - 7) * LANES + half]
    for p in range(PT):
        for t in range(TILES):
            rows_s[p * FRAMES : (p + 1) * FRAMES, t * LANES : (t + 1) * LANES] = wide_s[
                t, pl.ds(p, FRAMES, stride=PT), :
            ].astype(BF)
    all_t[...] = rows_s[...].T
    row_patch = lax.broadcasted_iota(jnp.int32, (BLOCK, BLOCK), 0) // FRAMES
    col_patch = lax.broadcasted_iota(jnp.int32, (BLOCK, BLOCK), 1) // FRAMES
    same = row_patch == col_patch
    for b in range(TOK // BLOCK):
        rows = slice(b * BLOCK, (b + 1) * BLOCK)
        for h in range(HEADS):
            at = [slice(i * W + h * HS, i * W + (h + 1) * HS) for i in range(4)]
            q_t, k_t, v_t, ga_t = [all_t[cols, rows] for cols in at]
            scores = dot(rows_s[rows, at[1]], q_t) * TEMPER
            scores = jnp.where(same, scores, -jnp.inf)
            powers = jnp.exp(scores - jnp.max(scores, axis=0, keepdims=True))
            probs = powers * (1.0 / jnp.sum(powers, axis=0, keepdims=True))
            weights = probs.astype(BF)
            g_t[at[3], rows] = dot(v_t, weights)
            grad_probs = dot(rows_s[rows, at[2]], ga_t)
            delta = jnp.sum(probs * grad_probs, axis=0, keepdims=True)
            grad_scores = (probs * (grad_probs - delta)).astype(BF)
            g_t[at[0], rows] = dot(k_t, grad_scores) * TEMPER
            g_t[at[1], rows] = dot_nt(q_t, grad_scores) * TEMPER
            g_t[at[2], rows] = dot_nt(ga_t, weights)
    for t in range(TILES):
        tile = g_t[t * LANES : (t + 1) * LANES, :].T
        for p in range(PT):
            wide_s[t, pl.ds(p, FRAMES, stride=PT), :] = tile[p * FRAMES : (p + 1) * FRAMES]
    for t in range(TILES):
        grads_ref[:, t * LANES : (t + 1) * LANES] = wide_s[t].astype(BF)
    copies[NX].wait()
    norm = dot(grads_ref[:, : 3 * W], wqkv_s[...])
    for at in range(NX):
        part = norm[:, at * W : (at + 1) * W].reshape(NT, 2 * PT, W)
        slot = lax.rem(at + NX - x_ref[0], NX)
        for f in range(FR):
            norm_s[slot, :, f * W : (f + 1) * W] = part[:, f * PT : (f + 1) * PT, :].reshape(NT * PT, W).astype(BF)
    for at in range(NX):
        norm_refs[at][...] = norm_s[at]


def attend(x, qkv, gon, w_ordered, w_qkv):
    scalar = pl.BlockSpec(memory_space=pltpu.SMEM)
    whole = pl.BlockSpec(memory_space=pltpu.VMEM)
    hbm = pl.BlockSpec(memory_space=pl.ANY)
    return call(
        attend_kernel,
        (jax.ShapeDtypeStruct((TOK, 4 * W), BF),) + (jax.ShapeDtypeStruct((TOK // 2, 2 * W), BF),) * NX,
        5_000_000_000,
        in_specs=[scalar, whole, hbm, whole, hbm],
        scratch_shapes=[
            pltpu.VMEM((TILES, TOK, LANES), F32),
            pltpu.VMEM((TOK, 4 * W), BF),
            pltpu.VMEM((4 * W, TOK), BF),
            pltpu.VMEM((4 * W, TOK), F32),
            pltpu.VMEM((NX, TOK // 2, 2 * W), BF),
            pltpu.VMEM((NX, NT, 2 * PT, GO), BF),
            pltpu.VMEM((3 * W, D), BF),
            pltpu.SemaphoreType.DMA((NX + 1,)),
        ],
    )(x, qkv, gon, w_ordered, w_qkv)


def weight_kernel(half_ref, gon_ref, grads_ref, *refs):
    del half_ref
    out_ref = refs[-1]
    gon_t = gon_ref[0].reshape(TOK, 2 * W).astype(F32).T.astype(BF)
    for rows, cols in ((slice(W, 2 * W), slice(0, 3 * W)), (slice(0, W), slice(3 * W, 4 * W))):
        total = dot(gon_t[rows], grads_ref[:, cols])
        if len(refs) == 2:
            total = total + refs[0][:, cols].astype(F32)
        out_ref[:, cols] = total.astype(BF)


def weight_half(half, gon, grads, *got):
    block = pl.BlockSpec((W, 4 * W), lambda j, half: (j, 0))
    spec = pltpu.PrefetchScalarGridSpec(
        num_scalar_prefetch=1,
        grid=(2,),
        in_specs=[
            pl.BlockSpec((1, NT, 2 * PT, 2 * W), lambda j, half: (half[0] * 2 + j, 0, 0, 0)),
            pl.BlockSpec((TOK, 4 * W), lambda j, half: (0, 0)),
        ]
        + [block] * len(got),
        out_specs=block,
    )
    shape = jax.ShapeDtypeStruct((2 * W, 4 * W), BF)
    return call(weight_kernel, shape, 4_000_000_000, spec)(half, gon, grads, *got)


def add_kernel(*refs):
    total = refs[0][...].astype(F32)
    for ref in refs[1:-1]:
        total = total + ref[...].astype(F32)
    refs[-1][...] = total.astype(BF)


def spread_kernel(x_ref, *refs):
    out_ref = refs[-1]
    for at in range(NX):
        for k in range(NX):

            @pl.when(lax.rem(x_ref[0] + NX - k, NX) == at)
            def _(at=at, k=k):
                for f in range(FR):
                    out_ref[f, :, at * W : (at + 1) * W] = refs[k][:, f * W : (f + 1) * W]


def total_kernel(in_ref, qkv_ref, out_ref):
    total = in_ref[0].astype(F32)
    for at in range(1, 8):
        total = total + in_ref[at].astype(F32)
    for i in range(3):
        qkv_ref[i] = total[:, i * W : (i + 1) * W]
    out_ref[...] = total[:, 3 * W :]


def shift(array, k):
    return lax.ppermute(array, "x", [(i, (i + k) % NX) for i in range(NX)])


def on_device(queries, key_vectors, value_vectors, normed, grad_output, w_qkv, w_out):
    order = jnp.asarray(feature_order())
    x = lax.axis_index("x")
    core = lax.axis_index("core")
    scalar = pl.BlockSpec(memory_space=pltpu.SMEM)
    whole = pl.BlockSpec(memory_space=pltpu.VMEM)
    gon = pick(x.reshape(1), order, grad_output[0], normed[0])
    gon = lax.all_to_all(gon, TM, 0, 0, tiled=True)
    gon = lax.all_gather(gon, "x", axis=0)
    qkv = call(pack_kernel, jax.ShapeDtypeStruct((NT, 2 * PT, 3 * W), BF), 30_000_000_000)(
        *[jnp.swapaxes(item[0], 1, 2) for item in (queries, key_vectors, value_vectors)]
    )
    qkv = lax.all_to_all(qkv, TM, 0, 0, tiled=True)
    w_ordered = call(reorder_kernel, jax.ShapeDtypeStruct((NX, W, W), BF), 1_000_000_000)(order, w_out)
    grads, *parts = attend(x.reshape(1), qkv, gon, w_ordered, jnp.swapaxes(w_qkv, 1, 2).reshape(3 * W, D))

    moved = [parts[0]] + [shift(parts[k], k) for k in range(1, NX)]
    sent = weight_half((1 - core).reshape(1), gon, grads)
    got = lax.ppermute(sent, "core", [(0, 1), (1, 0)])
    both = weight_half(core.reshape(1), gon, grads, got).reshape(4, D // 8, 4 * W)
    quarter = lax.psum_scatter(both, Y, scatter_dimension=0, tiled=True)

    own_norm = call(add_kernel, jax.ShapeDtypeStruct((TOK // 2, 2 * W), BF), 40_000_000_000)(*moved)
    own_norm = lax.all_to_all(own_norm.reshape(NT, PT, 2 * W), TM, 0, 0, tiled=True).reshape(TOK // 2, 2 * W)
    all_norm = [own_norm] + [shift(own_norm, k) for k in range(1, NX)]
    grad_normed = call(
        spread_kernel,
        jax.ShapeDtypeStruct((FR, TOK // 2, D), BF),
        40_000_000_000,
        in_specs=[scalar] + [whole] * NX,
    )(x.reshape(1), *all_norm)

    pieces = lax.all_to_all(quarter.reshape(8, 20, 4 * W), "z", 0, 0, tiled=True)
    grad_qkv, grad_out = call(
        total_kernel, (jax.ShapeDtypeStruct((3, 20, W), F32), jax.ShapeDtypeStruct((20, W), F32))
    )(pieces)
    return (grad_normed[None], grad_qkv, grad_out.T)


def solution(mesh):
    own = Mesh(mesh.devices.reshape(2, 8, 2, 2, 4), ("dp", "z", "yl", "core", "x"))
    in_specs = (
        P("dp", TM, None, "x"),
        P("dp", TM, None, "x"),
        P("dp", TM, None, "x"),
        P("dp", TM, None, None),
        P("dp", TM, None, None),
        P(None, None, "x"),
        P("x", None),
    )
    out_specs = (
        P("dp", TM, None, None),
        P(None, ("dp",) + TM, "x"),
        P("x", ("dp",) + TM),
    )
    return jax.shard_map(on_device, mesh=own, in_specs=in_specs, out_specs=out_specs, check_vma=False)
```

```python
import functools

import jax
import jax.numpy as jnp
import numpy as np
from jax import lax
from jax.experimental import pallas as pl
from jax.experimental.pallas import tpu as pltpu
from jax.sharding import Mesh
from jax.sharding import PartitionSpec as P

HS = 80
HEADS = 4
W = HEADS * HS
D = 1280
NX = 4
NT = 32
FR = 2
PT = 8
TOK = 512
FRAMES = 64
LANES = 128
STEPS = 2
GO = 384
TILES = 4 * W // LANES
HALF_TILES = 5
BLOCK = 256
TEMPER = HS ** (-0.5)
TM = ("z", "yl", "core")
Y = ("dp", "yl")
BF = jnp.bfloat16
F32 = jnp.float32
LIMIT = 48 * 1024 * 1024


def feature_order():
    order = np.zeros(D, np.int32)
    at = 0
    for core in range(2):
        for y in range(4):
            for z in range(8):
                dp, yl = divmod(y, 2)
                start = (((dp * 8 + z) * 2 + yl) * 2 + core) * 20
                order[at : at + 20] = np.arange(start, start + 20)
                at += 20
    return order.reshape(NX, 1, W)


def dot(a, b):
    return lax.dot_general(a, b, (((1,), (0,)), ((), ())), preferred_element_type=F32)


def dot_nt(a, b):
    return lax.dot_general(a, b, (((1,), (1,)), ((), ())), preferred_element_type=F32)


def call(kernel, out_shape, flops=0, grid_spec=None, limit=LIMIT, **kw):
    params = pltpu.CompilerParams(vmem_limit_bytes=limit)
    cost = pl.CostEstimate(flops=flops, bytes_accessed=4_000_000, transcendentals=0)
    if grid_spec is not None:
        kw["grid_spec"] = grid_spec
    return pl.pallas_call(kernel, out_shape=out_shape, compiler_params=params, cost_estimate=cost, **kw)


def to_chunks(rows):
    width = rows.shape[-1]
    half = rows.shape[0] // 2
    low = rows[:half].reshape(-1, PT, width)
    high = rows[half:].reshape(-1, PT, width)
    return jnp.concatenate([low, high], axis=1).astype(BF)


def one_hot(feat, among):
    places = lax.broadcasted_iota(jnp.int32, (among, W), 0)
    return jnp.where(places == feat, 1.0, 0.0).astype(BF)


def pick_kernel(x_ref, order_ref, go_hbm, n_hbm, out_hbm, rows_s, out_s, sems, out_sems):
    part = NT * PT // STEPS
    first = lax.rem(x_ref[0], 2) * (D // 2)
    fetches = [
        [
            pltpu.make_async_copy(
                hbm.at[f, pl.ds(i * part, part), pl.ds(pl.multiple_of(first, LANES), D // 2)],
                rows_s.at[at, i, f],
                sems.at[(at * STEPS + i) * FR + f],
            )
            for at, hbm in enumerate((go_hbm, n_hbm))
            for f in range(FR)
        ]
        for i in range(STEPS)
    ]
    for group in fetches:
        for fetch in group:
            fetch.start()
    pick = one_hot(order_ref[x_ref[0]] - first, D // 2)
    chunks = NT // STEPS
    stores = []
    for i in range(STEPS):
        for fetch in fetches[i]:
            fetch.wait()
        for at in range(2):
            rows = dot(rows_s[at, i].reshape(FR * part, D // 2), pick)
            out_s[i * chunks : (i + 1) * chunks, :, at * W : (at + 1) * W] = to_chunks(rows)
        own = pl.ds(i * chunks, chunks)
        stores.append(pltpu.make_async_copy(out_s.at[own], out_hbm.at[own], out_sems.at[i]))
        stores[-1].start()
    for store in stores:
        store.wait()


def pick(x, order, grad_output, normed):
    hbm = pl.BlockSpec(memory_space=pl.ANY)
    shape = (NT, 2 * PT, 2 * W)
    return call(
        pick_kernel,
        jax.ShapeDtypeStruct(shape, BF),
        850_000_000,
        limit=60 * 1024 * 1024,
        in_specs=[
            pl.BlockSpec(memory_space=pltpu.SMEM),
            pl.BlockSpec(memory_space=pltpu.VMEM),
            hbm,
            hbm,
        ],
        out_specs=hbm,
        scratch_shapes=[
            pltpu.VMEM((2, STEPS, FR, NT * PT // STEPS, D // 2), BF),
            pltpu.VMEM(shape, BF),
            pltpu.SemaphoreType.DMA((2 * STEPS * FR,)),
            pltpu.SemaphoreType.DMA((STEPS,)),
        ],
    )(x, order, grad_output, normed)


def pack_kernel(q_ref, k_ref, v_ref, out_ref):
    packed = [
        ref[...].reshape(FR * W, NT * PT).astype(F32).T.reshape(NT, PT, FR * W) for ref in (q_ref, k_ref, v_ref)
    ]
    out_ref[...] = jnp.concatenate(packed, axis=1).astype(BF)


def reorder_kernel(feat_ref, w_ref, out_ref):
    for at in range(NX):
        out_ref[at] = dot(w_ref[...], one_hot(feat_ref[at], D)).astype(BF)


def place(p, f):
    return (p // 4) * BLOCK + f * (BLOCK // 2) + (p % 4) * NT


def attend_kernel(x_ref, qkv_ref, gon_ref, wout_ref, wqkv_hbm, grads_ref, *rest):
    norm_refs, (wide_s, rows_s, v_s, qkvg_t, g_t, norm_s, go_s, wqkv_s, sems) = rest[:NX], rest[NX:]
    copies = [
        pltpu.make_async_copy(gon_ref.at[at, :, :, pl.ds(0, GO)], go_s.at[at], sems.at[at]) for at in range(NX)
    ]
    copies.append(pltpu.make_async_copy(wqkv_hbm, wqkv_s, sems.at[NX]))
    for copy in copies:
        copy.start()
    half = BLOCK // 2
    values = qkv_ref[...].astype(F32)
    for a in range(3):
        own = values[:, a * PT : (a + 1) * PT, :].reshape(NT * PT, FR * W)
        for t in range(HALF_TILES):
            wide_s[t, : NT * PT, :] = own[:, t * LANES : (t + 1) * LANES]
        for p in range(PT):
            for t in range(HALF_TILES):
                rows_s[p * NT : (p + 1) * NT, t * LANES : (t + 1) * LANES] = wide_s[t, pl.ds(p, NT, stride=PT), :]
        rows = rows_s[...]
        if a > 0:
            v_s[a - 1] = rows.astype(BF)
        turned = rows.T.astype(BF)
        for b in range(TOK // BLOCK):
            for f in range(FR):
                start = b * BLOCK + f * half
                qkvg_t[a * W : (a + 1) * W, start : start + half] = turned[
                    f * W : (f + 1) * W, b * half : (b + 1) * half
                ]
    acc = jnp.zeros((TOK, W), F32)
    for at in range(NX):
        copies[at].wait()
        acc = acc + dot_nt(go_s[at].reshape(TOK, GO)[:, :W], wout_ref[at])
    wide_s[0] = acc[:, :LANES]
    wide_s[1] = acc[:, LANES : 2 * LANES]
    wide_s[2, :, : W - 2 * LANES] = acc[:, 2 * LANES :]
    for p in range(PT):
        for f in range(FR):
            at = place(p, f)
            for t in range(3):
                wide = min(LANES, W - t * LANES)
                piece = wide_s[t, pl.ds(f * PT + p, NT, stride=FR * PT), :]
                g_t[at : at + NT, t * LANES : t * LANES + wide] = piece[:, :wide]
    qkvg_t[3 * W :, :] = g_t[:TOK, :W].T.astype(BF)
    row_patch = lax.broadcasted_iota(jnp.int32, (BLOCK, BLOCK), 0) // NT % 4
    col_patch = lax.broadcasted_iota(jnp.int32, (BLOCK, BLOCK), 1) // NT % 4
    same = row_patch == col_patch
    for b in range(TOK // BLOCK):
        cols = slice(b * BLOCK, (b + 1) * BLOCK)
        own = slice(b * half, (b + 1) * half)
        for h in range(HEADS):
            heads = [slice(i * W + h * HS, i * W + (h + 1) * HS) for i in range(4)]
            q_t, k_t, v_t, ga_t = [qkvg_t[head, cols] for head in heads]
            k_rows, v_rows = [
                jnp.concatenate([v_s[i, own, heads[f]] for f in range(FR)], axis=0) for i in range(2)
            ]
            scores = dot(k_rows, q_t) * TEMPER
            scores = jnp.where(same, scores, -jnp.inf)
            powers = jnp.exp(scores - jnp.max(scores, axis=0, keepdims=True))
            probs = powers * (1.0 / jnp.sum(powers, axis=0, keepdims=True))
            weights = probs.astype(BF)
            g_t[heads[3], cols] = dot(v_t, weights)
            grad_probs = dot(v_rows, ga_t)
            delta = jnp.sum(probs * grad_probs, axis=0, keepdims=True)
            grad_scores = (probs * (grad_probs - delta)).astype(BF)
            g_t[heads[0], cols] = dot(k_t, grad_scores) * TEMPER
            g_t[heads[1], cols] = dot_nt(q_t, grad_scores) * TEMPER
            g_t[heads[2], cols] = dot_nt(ga_t, weights)
    for t in range(TILES):
        tile = g_t[t * LANES : (t + 1) * LANES, :].T
        for p in range(PT):
            for f in range(FR):
                at = place(p, f)
                wide_s[t, pl.ds(f * PT + p, NT, stride=FR * PT), :] = tile[at : at + NT]
    for t in range(TILES):
        grads_ref[:, t * LANES : (t + 1) * LANES] = wide_s[t].astype(BF)
    copies[NX].wait()
    norm = dot(grads_ref[:, : 3 * W], wqkv_s[...])
    for at in range(NX):
        part = norm[:, at * W : (at + 1) * W].reshape(NT, 2 * PT, W)
        slot = lax.rem(at + NX - x_ref[0], NX)
        for f in range(FR):
            norm_s[slot, :, f * W : (f + 1) * W] = part[:, f * PT : (f + 1) * PT, :].reshape(NT * PT, W).astype(BF)
    for at in range(NX):
        norm_refs[at][...] = norm_s[at]


def attend(x, qkv, gon, w_ordered, w_qkv):
    scalar = pl.BlockSpec(memory_space=pltpu.SMEM)
    whole = pl.BlockSpec(memory_space=pltpu.VMEM)
    hbm = pl.BlockSpec(memory_space=pl.ANY)
    return call(
        attend_kernel,
        (jax.ShapeDtypeStruct((TOK, 4 * W), BF),) + (jax.ShapeDtypeStruct((TOK // 2, 2 * W), BF),) * NX,
        5_000_000_000,
        in_specs=[scalar, whole, hbm, whole, hbm],
        scratch_shapes=[
            pltpu.VMEM((TILES, TOK, LANES), F32),
            pltpu.VMEM((NT * PT, FR * W), F32),
            pltpu.VMEM((2, NT * PT, FR * W), BF),
            pltpu.VMEM((4 * W, TOK), BF),
            pltpu.VMEM((4 * W, TOK), F32),
            pltpu.VMEM((NX, TOK // 2, 2 * W), BF),
            pltpu.VMEM((NX, NT, 2 * PT, GO), BF),
            pltpu.VMEM((3 * W, D), BF),
            pltpu.SemaphoreType.DMA((NX + 1,)),
        ],
    )(x, qkv, gon, w_ordered, w_qkv)


def weight_kernel(half_ref, gon_ref, grads_ref, *refs):
    del half_ref
    out_ref = refs[-1]
    gon_t = gon_ref[0].reshape(TOK, 2 * W).astype(F32).T.astype(BF)
    for rows, cols in ((slice(W, 2 * W), slice(0, 3 * W)), (slice(0, W), slice(3 * W, 4 * W))):
        total = dot(gon_t[rows], grads_ref[:, cols])
        if len(refs) == 2:
            total = total + refs[0][:, cols].astype(F32)
        out_ref[:, cols] = total.astype(BF)


def weight_half(half, gon, grads, *got):
    block = pl.BlockSpec((W, 4 * W), lambda j, half: (j, 0))
    spec = pltpu.PrefetchScalarGridSpec(
        num_scalar_prefetch=1,
        grid=(2,),
        in_specs=[
            pl.BlockSpec((1, NT, 2 * PT, 2 * W), lambda j, half: (half[0] * 2 + j, 0, 0, 0)),
            pl.BlockSpec((TOK, 4 * W), lambda j, half: (0, 0)),
        ]
        + [block] * len(got),
        out_specs=block,
    )
    shape = jax.ShapeDtypeStruct((2 * W, 4 * W), BF)
    return call(weight_kernel, shape, 4_000_000_000, spec)(half, gon, grads, *got)


def add_kernel(*refs):
    total = refs[0][...].astype(F32)
    for ref in refs[1:-1]:
        total = total + ref[...].astype(F32)
    refs[-1][...] = total.astype(BF)


def spread_kernel(x_ref, *refs):
    out_ref = refs[-1]
    for at in range(NX):
        for k in range(NX):

            @pl.when(lax.rem(x_ref[0] + NX - k, NX) == at)
            def _(at=at, k=k):
                for f in range(FR):
                    out_ref[f, :, at * W : (at + 1) * W] = refs[k][:, f * W : (f + 1) * W]


def regroup_kernel(in_ref, out_ref):
    rows = in_ref[...].astype(F32)
    for at in range(8):
        out_ref[at] = rows[at * 20 : (at + 1) * 20].astype(BF)


def total_kernel(in_ref, qkv_ref, out_ref):
    total = in_ref[0].astype(F32)
    for at in range(1, 8):
        total = total + in_ref[at].astype(F32)
    for i in range(3):
        qkv_ref[i] = total[:, i * W : (i + 1) * W]
    out_ref[...] = total[:, 3 * W :]


def shift(array, k):
    return lax.ppermute(array, "x", [(i, (i + k) % NX) for i in range(NX)])


def on_device(queries, key_vectors, value_vectors, normed, grad_output, w_qkv, w_out):
    order = jnp.asarray(feature_order())
    x = lax.axis_index("x")
    core = lax.axis_index("core")
    scalar = pl.BlockSpec(memory_space=pltpu.SMEM)
    whole = pl.BlockSpec(memory_space=pltpu.VMEM)
    gon = pick(x.reshape(1), order, grad_output[0], normed[0])
    gon = lax.all_to_all(gon, TM, 0, 0, tiled=True)
    gon = lax.all_gather(gon, "x", axis=0)
    qkv = call(pack_kernel, jax.ShapeDtypeStruct((NT, 3 * PT, FR * W), BF), 30_000_000_000)(
        *[jnp.swapaxes(item[0], 1, 2) for item in (queries, key_vectors, value_vectors)]
    )
    qkv = lax.all_to_all(qkv, TM, 0, 0, tiled=True)
    w_ordered = call(reorder_kernel, jax.ShapeDtypeStruct((NX, W, W), BF), 1_000_000_000)(order, w_out)
    grads, *parts = attend(x.reshape(1), qkv, gon, w_ordered, jnp.swapaxes(w_qkv, 1, 2).reshape(3 * W, D))

    moved = [parts[0]] + [shift(parts[k], k) for k in range(1, NX)]
    sent = weight_half((1 - core).reshape(1), gon, grads)
    got = lax.ppermute(sent, "core", [(0, 1), (1, 0)])
    both = weight_half(core.reshape(1), gon, grads, got).reshape(4, D // 8, 4 * W)
    quarter = lax.psum_scatter(both, Y, scatter_dimension=0, tiled=True)

    own_norm = call(add_kernel, jax.ShapeDtypeStruct((TOK // 2, 2 * W), BF), 40_000_000_000)(*moved)
    own_norm = lax.all_to_all(own_norm.reshape(NT, PT, 2 * W), TM, 0, 0, tiled=True).reshape(TOK // 2, 2 * W)
    all_norm = [own_norm] + [shift(own_norm, k) for k in range(1, NX)]
    grad_normed = call(
        spread_kernel,
        jax.ShapeDtypeStruct((FR, TOK // 2, D), BF),
        40_000_000_000,
        in_specs=[scalar] + [whole] * NX,
    )(x.reshape(1), *all_norm)

    pieces = call(regroup_kernel, jax.ShapeDtypeStruct((8, 20, 4 * W), BF), limit=60 * 1024 * 1024)(quarter.reshape(D // 8, 4 * W))
    pieces = lax.all_to_all(pieces, "z", 0, 0, tiled=True)
    grad_qkv, grad_out = call(
        total_kernel, (jax.ShapeDtypeStruct((3, 20, W), F32), jax.ShapeDtypeStruct((20, W), F32))
    )(pieces)
    return (grad_normed[None], grad_qkv, grad_out.T)


def solution(mesh):
    own = Mesh(mesh.devices.reshape(2, 8, 2, 2, 4), ("dp", "z", "yl", "core", "x"))
    in_specs = (
        P("dp", TM, None, "x"),
        P("dp", TM, None, "x"),
        P("dp", TM, None, "x"),
        P("dp", TM, None, None),
        P("dp", TM, None, None),
        P(None, None, "x"),
        P("x", None),
    )
    out_specs = (
        P("dp", TM, None, None),
        P(None, ("dp",) + TM, "x"),
        P("x", ("dp",) + TM),
    )
    return jax.shard_map(on_device, mesh=own, in_specs=in_specs, out_specs=out_specs, check_vma=False)
```

```python
import functools

import jax
import jax.numpy as jnp
import numpy as np
from jax import lax
from jax.experimental import pallas as pl
from jax.experimental.pallas import tpu as pltpu
from jax.sharding import Mesh
from jax.sharding import PartitionSpec as P

HS = 80
HEADS = 4
W = HEADS * HS
D = 1280
NX = 4
NT = 32
FR = 2
PT = 8
TOK = 512
FRAMES = 64
LANES = 128
STEPS = 2
GO = 384
TILES = 4 * W // LANES
HALF_TILES = 5
BLOCK = 256
TEMPER = HS ** (-0.5)
TM = ("z", "yl", "core")
Y = ("dp", "yl")
BF = jnp.bfloat16
F32 = jnp.float32
LIMIT = 24 * 1024 * 1024


def feature_order():
    order = np.zeros(D, np.int32)
    at = 0
    for core in range(2):
        for y in range(4):
            for z in range(8):
                dp, yl = divmod(y, 2)
                start = (((dp * 8 + z) * 2 + yl) * 2 + core) * 20
                order[at : at + 20] = np.arange(start, start + 20)
                at += 20
    return order.reshape(NX, 1, W)


def dot(a, b):
    return lax.dot_general(a, b, (((1,), (0,)), ((), ())), preferred_element_type=F32)


def dot_nt(a, b):
    return lax.dot_general(a, b, (((1,), (1,)), ((), ())), preferred_element_type=F32)


def call(kernel, out_shape, flops=0, grid_spec=None, limit=LIMIT, **kw):
    params = pltpu.CompilerParams(vmem_limit_bytes=limit)
    cost = pl.CostEstimate(flops=flops, bytes_accessed=4_000_000, transcendentals=0)
    if grid_spec is not None:
        kw["grid_spec"] = grid_spec
    return pl.pallas_call(kernel, out_shape=out_shape, compiler_params=params, cost_estimate=cost, **kw)


def to_chunks(rows):
    width = rows.shape[-1]
    half = rows.shape[0] // 2
    low = rows[:half].reshape(-1, PT, width)
    high = rows[half:].reshape(-1, PT, width)
    return jnp.concatenate([low, high], axis=1).astype(BF)


def one_hot(feat, among):
    places = lax.broadcasted_iota(jnp.int32, (among, W), 0)
    return jnp.where(places == feat, 1.0, 0.0).astype(BF)


def pick_kernel(x_ref, order_ref, go_hbm, n_hbm, out_hbm, rows_s, out_s, sems, out_sems):
    part = NT * PT // STEPS
    first = lax.rem(x_ref[0], 2) * (D // 2)
    fetches = [
        [
            pltpu.make_async_copy(
                hbm.at[f, pl.ds(i * part, part), pl.ds(pl.multiple_of(first, LANES), D // 2)],
                rows_s.at[at, i, f],
                sems.at[(at * STEPS + i) * FR + f],
            )
            for at, hbm in enumerate((go_hbm, n_hbm))
            for f in range(FR)
        ]
        for i in range(STEPS)
    ]
    for group in fetches:
        for fetch in group:
            fetch.start()
    pick = one_hot(order_ref[x_ref[0]] - first, D // 2)
    chunks = NT // STEPS
    stores = []
    for i in range(STEPS):
        for fetch in fetches[i]:
            fetch.wait()
        for at in range(2):
            rows = dot(rows_s[at, i].reshape(FR * part, D // 2), pick)
            out_s[i * chunks : (i + 1) * chunks, :, at * W : (at + 1) * W] = to_chunks(rows)
        own = pl.ds(i * chunks, chunks)
        stores.append(pltpu.make_async_copy(out_s.at[own], out_hbm.at[own], out_sems.at[i]))
        stores[-1].start()
    for store in stores:
        store.wait()


def pick(x, order, grad_output, normed):
    hbm = pl.BlockSpec(memory_space=pl.ANY)
    shape = (NT, 2 * PT, 2 * W)
    return call(
        pick_kernel,
        jax.ShapeDtypeStruct(shape, BF),
        850_000_000,
        limit=60 * 1024 * 1024,
        in_specs=[
            pl.BlockSpec(memory_space=pltpu.SMEM),
            pl.BlockSpec(memory_space=pltpu.VMEM),
            hbm,
            hbm,
        ],
        out_specs=hbm,
        scratch_shapes=[
            pltpu.VMEM((2, STEPS, FR, NT * PT // STEPS, D // 2), BF),
            pltpu.VMEM(shape, BF),
            pltpu.SemaphoreType.DMA((2 * STEPS * FR,)),
            pltpu.SemaphoreType.DMA((STEPS,)),
        ],
    )(x, order, grad_output, normed)


def pack_kernel(q_ref, k_ref, v_ref, out_ref):
    packed = [
        ref[...].reshape(FR * W, NT * PT).astype(F32).T.reshape(NT, PT, FR * W) for ref in (q_ref, k_ref, v_ref)
    ]
    out_ref[...] = jnp.concatenate(packed, axis=1).astype(BF)


def reorder_kernel(feat_ref, w_ref, out_ref):
    for at in range(NX):
        out_ref[at] = dot(w_ref[...], one_hot(feat_ref[at], D)).astype(BF)


def place(p, f):
    return (p // 4) * BLOCK + f * (BLOCK // 2) + (p % 4) * NT


def attend_kernel(x_ref, qkv_ref, own_hbm, left_hbm, right_hbm, low_hbm, high_hbm, wout_ref, wqkv_hbm, grads_ref, *rest):
    norm_refs, (wide_s, rows_s, v_s, qkvg_t, g_t, norm_s, go_s, wqkv_s, sems) = rest[:NX], rest[NX:]
    cols = pl.ds(0, GO)
    copies = [
        pltpu.make_async_copy(hbm.at[:, :, cols], go_s.at[at], sems.at[at])
        for at, hbm in enumerate((own_hbm, left_hbm, right_hbm))
    ]
    copies += [
        pltpu.make_async_copy(hbm.at[:, :, cols], go_s.at[3, pl.ds(i * NT // 2, NT // 2)], sems.at[3 + i])
        for i, hbm in enumerate((low_hbm, high_hbm))
    ]
    copies.append(pltpu.make_async_copy(wqkv_hbm, wqkv_s, sems.at[5]))
    for copy in copies:
        copy.start()
    half = BLOCK // 2
    values = qkv_ref[...].astype(F32)
    for a in range(3):
        own = values[:, a * PT : (a + 1) * PT, :].reshape(NT * PT, FR * W)
        for t in range(HALF_TILES):
            wide_s[t, : NT * PT, :] = own[:, t * LANES : (t + 1) * LANES]
        for p in range(PT):
            for t in range(HALF_TILES):
                rows_s[p * NT : (p + 1) * NT, t * LANES : (t + 1) * LANES] = wide_s[t, pl.ds(p, NT, stride=PT), :]
        rows = rows_s[...]
        if a > 0:
            v_s[a - 1] = rows.astype(BF)
        turned = rows.T.astype(BF)
        for b in range(TOK // BLOCK):
            for f in range(FR):
                start = b * BLOCK + f * half
                qkvg_t[a * W : (a + 1) * W, start : start + half] = turned[
                    f * W : (f + 1) * W, b * half : (b + 1) * half
                ]
    acc = jnp.zeros((TOK, W), F32)
    for at, needed, behind in ((0, (0,), 0), (1, (1,), 1), (2, (2,), 3), (3, (3, 4), 2)):
        for i in needed:
            copies[i].wait()
        block = lax.rem(x_ref[0] + NX - behind, NX)
        acc = acc + dot_nt(go_s[at].reshape(TOK, GO)[:, :W], wout_ref[block])
    wide_s[0] = acc[:, :LANES]
    wide_s[1] = acc[:, LANES : 2 * LANES]
    wide_s[2, :, : W - 2 * LANES] = acc[:, 2 * LANES :]
    for p in range(PT):
        for f in range(FR):
            at = place(p, f)
            for t in range(3):
                wide = min(LANES, W - t * LANES)
                piece = wide_s[t, pl.ds(f * PT + p, NT, stride=FR * PT), :]
                g_t[at : at + NT, t * LANES : t * LANES + wide] = piece[:, :wide]
    qkvg_t[3 * W :, :] = g_t[:TOK, :W].T.astype(BF)
    row_patch = lax.broadcasted_iota(jnp.int32, (BLOCK, BLOCK), 0) // NT % 4
    col_patch = lax.broadcasted_iota(jnp.int32, (BLOCK, BLOCK), 1) // NT % 4
    same = row_patch == col_patch
    for b in range(TOK // BLOCK):
        cols = slice(b * BLOCK, (b + 1) * BLOCK)
        own = slice(b * half, (b + 1) * half)
        for h in range(HEADS):
            heads = [slice(i * W + h * HS, i * W + (h + 1) * HS) for i in range(4)]
            q_t, k_t, v_t, ga_t = [qkvg_t[head, cols] for head in heads]
            k_rows, v_rows = [
                jnp.concatenate([v_s[i, own, heads[f]] for f in range(FR)], axis=0) for i in range(2)
            ]
            scores = dot(k_rows, q_t) * TEMPER
            scores = jnp.where(same, scores, -jnp.inf)
            powers = jnp.exp(scores - jnp.max(scores, axis=0, keepdims=True))
            probs = powers * (1.0 / jnp.sum(powers, axis=0, keepdims=True))
            weights = probs.astype(BF)
            g_t[heads[3], cols] = dot(v_t, weights)
            grad_probs = dot(v_rows, ga_t)
            delta = jnp.sum(probs * grad_probs, axis=0, keepdims=True)
            grad_scores = (probs * (grad_probs - delta)).astype(BF)
            g_t[heads[0], cols] = dot(k_t, grad_scores) * TEMPER
            g_t[heads[1], cols] = dot_nt(q_t, grad_scores) * TEMPER
            g_t[heads[2], cols] = dot_nt(ga_t, weights)
    for t in range(TILES):
        tile = g_t[t * LANES : (t + 1) * LANES, :].T
        for p in range(PT):
            for f in range(FR):
                at = place(p, f)
                wide_s[t, pl.ds(f * PT + p, NT, stride=FR * PT), :] = tile[at : at + NT]
    for t in range(TILES):
        grads_ref[:, t * LANES : (t + 1) * LANES] = wide_s[t].astype(BF)
    copies[5].wait()
    norm = dot(grads_ref[:, : 3 * W], wqkv_s[...])
    for at in range(NX):
        part = norm[:, at * W : (at + 1) * W].reshape(NT, 2 * PT, W)
        slot = lax.rem(at + NX - x_ref[0], NX)
        for f in range(FR):
            norm_s[slot, :, f * W : (f + 1) * W] = part[:, f * PT : (f + 1) * PT, :].reshape(NT * PT, W).astype(BF)
    for at in range(NX):
        norm_refs[at][...] = norm_s[at]


def attend(x, qkv, gon, w_ordered, w_qkv):
    scalar = pl.BlockSpec(memory_space=pltpu.SMEM)
    whole = pl.BlockSpec(memory_space=pltpu.VMEM)
    hbm = pl.BlockSpec(memory_space=pl.ANY)
    return call(
        attend_kernel,
        (jax.ShapeDtypeStruct((TOK, 4 * W), BF),) + (jax.ShapeDtypeStruct((TOK // 2, 2 * W), BF),) * NX,
        5_000_000_000,
        in_specs=[scalar, whole] + [hbm] * 5 + [whole, hbm],
        scratch_shapes=[
            pltpu.VMEM((TILES, TOK, LANES), F32),
            pltpu.VMEM((NT * PT, FR * W), F32),
            pltpu.VMEM((2, NT * PT, FR * W), BF),
            pltpu.VMEM((4 * W, TOK), BF),
            pltpu.VMEM((4 * W, TOK), F32),
            pltpu.VMEM((NX, TOK // 2, 2 * W), BF),
            pltpu.VMEM((NX, NT, 2 * PT, GO), BF),
            pltpu.VMEM((3 * W, D), BF),
            pltpu.SemaphoreType.DMA((6,)),
        ],
    )(x, qkv, *gon, w_ordered, w_qkv)


def weight_kernel(place_ref, own_hbm, left_hbm, right_hbm, low_hbm, high_hbm, grads_ref, *refs):
    got_refs, (out_hbm, gon_s, out_s, sems, out_sems) = refs[:-5], refs[-5:]
    near = ((own_hbm, 0), (left_hbm, 3), (right_hbm, 1))
    for j in range(2):
        ahead = lax.rem(place_ref[1] * 2 + j + NX - place_ref[0], NX)
        for hbm, distance in near:

            @pl.when(ahead == distance)
            def _(hbm=hbm, j=j):
                pltpu.make_async_copy(hbm, gon_s.at[j], sems.at[j]).start()

        @pl.when(ahead == 2)
        def _(j=j):
            for i, hbm in enumerate((low_hbm, high_hbm)):
                pltpu.make_async_copy(hbm, gon_s.at[j, pl.ds(i * NT // 2, NT // 2)], sems.at[j]).start()

    stores = []
    for j in range(2):
        pltpu.make_async_copy(own_hbm, gon_s.at[j], sems.at[j]).wait()
        gon_t = gon_s[j].reshape(TOK, 2 * W).astype(F32).T.astype(BF)
        own = slice(j * W, (j + 1) * W)
        for rows, cols in ((slice(W, 2 * W), slice(0, 3 * W)), (slice(0, W), slice(3 * W, 4 * W))):
            total = dot(gon_t[rows], grads_ref[:, cols])
            for got_ref in got_refs:
                total = total + got_ref[own, cols].astype(F32)
            out_s[own, cols] = total.astype(BF)
        rows = pl.ds(j * W, W)
        stores.append(pltpu.make_async_copy(out_s.at[rows], out_hbm.at[rows], out_sems.at[j]))
        stores[-1].start()
    for store in stores:
        store.wait()


def weight_half(place, gon, grads, *got):
    whole = pl.BlockSpec(memory_space=pltpu.VMEM)
    hbm = pl.BlockSpec(memory_space=pl.ANY)
    shape = (2 * W, 4 * W)
    return call(
        weight_kernel,
        jax.ShapeDtypeStruct(shape, BF),
        4_000_000_000,
        in_specs=[pl.BlockSpec(memory_space=pltpu.SMEM)] + [hbm] * 5 + [whole] * (1 + len(got)),
        out_specs=hbm,
        scratch_shapes=[
            pltpu.VMEM((2, NT, 2 * PT, 2 * W), BF),
            pltpu.VMEM(shape, BF),
            pltpu.SemaphoreType.DMA((2,)),
            pltpu.SemaphoreType.DMA((2,)),
        ],
    )(place, *gon, grads, *got)


def add_kernel(*refs):
    total = refs[0][...].astype(F32)
    for ref in refs[1:-1]:
        total = total + ref[...].astype(F32)
    refs[-1][...] = total.astype(BF)


def spread_kernel(x_ref, *refs):
    out_ref = refs[-1]
    for at in range(NX):
        for k in range(NX):

            @pl.when(lax.rem(x_ref[0] + NX - k, NX) == at)
            def _(at=at, k=k):
                for f in range(FR):
                    out_ref[f, :, at * W : (at + 1) * W] = refs[k][:, f * W : (f + 1) * W]


def regroup_kernel(in_ref, out_ref):
    rows = in_ref[...].astype(F32)
    for at in range(8):
        out_ref[at] = rows[at * 20 : (at + 1) * 20].astype(BF)


def total_kernel(in_ref, qkv_ref, out_ref):
    total = in_ref[0].astype(F32)
    for at in range(1, 8):
        total = total + in_ref[at].astype(F32)
    for i in range(3):
        qkv_ref[i] = total[:, i * W : (i + 1) * W]
    out_ref[...] = total[:, 3 * W :]


def shift(array, k):
    return lax.ppermute(array, "x", [(i, (i + k) % NX) for i in range(NX)])


def on_device(queries, key_vectors, value_vectors, normed, grad_output, w_qkv, w_out):
    order = jnp.asarray(feature_order())
    x = lax.axis_index("x")
    core = lax.axis_index("core")
    scalar = pl.BlockSpec(memory_space=pltpu.SMEM)
    whole = pl.BlockSpec(memory_space=pltpu.VMEM)
    gon = pick(x.reshape(1), order, grad_output[0], normed[0])
    gon = lax.all_to_all(gon, TM, 0, 0, tiled=True)
    left, right = shift(gon, 1), shift(gon, NX - 1)
    low, high = shift(left[: NT // 2], 1), shift(right[NT // 2 :], NX - 1)
    gon = (gon, left, right, low, high)
    qkv = call(pack_kernel, jax.ShapeDtypeStruct((NT, 3 * PT, FR * W), BF), 30_000_000_000)(
        *[jnp.swapaxes(item[0], 1, 2) for item in (queries, key_vectors, value_vectors)]
    )
    qkv = lax.all_to_all(qkv, TM, 0, 0, tiled=True)
    w_ordered = call(reorder_kernel, jax.ShapeDtypeStruct((NX, W, W), BF), 1_000_000_000)(order, w_out)
    grads, *parts = attend(x.reshape(1), qkv, gon, w_ordered, jnp.swapaxes(w_qkv, 1, 2).reshape(3 * W, D))

    moved = [parts[0]] + [shift(parts[k], k) for k in range(1, NX)]
    sent = weight_half(jnp.stack([x, 1 - core]), gon, grads)
    got = lax.ppermute(sent, "core", [(0, 1), (1, 0)])
    both = weight_half(jnp.stack([x, core]), gon, grads, got).reshape(4, D // 8, 4 * W)
    quarter = lax.psum_scatter(both, Y, scatter_dimension=0, tiled=True)

    own_norm = call(add_kernel, jax.ShapeDtypeStruct((TOK // 2, 2 * W), BF), 40_000_000_000)(*moved)
    own_norm = lax.all_to_all(own_norm.reshape(NT, PT, 2 * W), TM, 0, 0, tiled=True).reshape(TOK // 2, 2 * W)
    all_norm = [own_norm] + [shift(own_norm, k) for k in range(1, NX)]
    grad_normed = call(
        spread_kernel,
        jax.ShapeDtypeStruct((FR, TOK // 2, D), BF),
        40_000_000_000,
        in_specs=[scalar] + [whole] * NX,
    )(x.reshape(1), *all_norm)

    pieces = call(regroup_kernel, jax.ShapeDtypeStruct((8, 20, 4 * W), BF), limit=60 * 1024 * 1024)(quarter.reshape(D // 8, 4 * W))
    pieces = lax.all_to_all(pieces, "z", 0, 0, tiled=True)
    grad_qkv, grad_out = call(
        total_kernel, (jax.ShapeDtypeStruct((3, 20, W), F32), jax.ShapeDtypeStruct((20, W), F32))
    )(pieces)
    return (grad_normed[None], grad_qkv, grad_out.T)


def solution(mesh):
    own = Mesh(mesh.devices.reshape(2, 8, 2, 2, 4), ("dp", "z", "yl", "core", "x"))
    in_specs = (
        P("dp", TM, None, "x"),
        P("dp", TM, None, "x"),
        P("dp", TM, None, "x"),
        P("dp", TM, None, None),
        P("dp", TM, None, None),
        P(None, None, "x"),
        P("x", None),
    )
    out_specs = (
        P("dp", TM, None, None),
        P(None, ("dp",) + TM, "x"),
        P("x", ("dp",) + TM),
    )
    return jax.shard_map(on_device, mesh=own, in_specs=in_specs, out_specs=out_specs, check_vma=False)
```

```python
import functools

import jax
import jax.numpy as jnp
import numpy as np
from jax import lax
from jax.experimental import pallas as pl
from jax.experimental.pallas import tpu as pltpu
from jax.sharding import Mesh
from jax.sharding import PartitionSpec as P

HS = 80
HEADS = 4
W = HEADS * HS
D = 1280
NX = 4
NT = 32
FR = 2
PT = 8
TOK = 512
FRAMES = 64
LANES = 128
STEPS = 2
GO = 384
TILES = 4 * W // LANES
HALF_TILES = 5
BLOCK = 256
TEMPER = HS ** (-0.5)
TM = ("z", "yl", "core")
Y = ("dp", "yl")
BF = jnp.bfloat16
F32 = jnp.float32
LIMIT = 48 * 1024 * 1024


def feature_order():
    order = np.zeros(D, np.int32)
    at = 0
    for core in range(2):
        for y in range(4):
            for z in range(8):
                dp, yl = divmod(y, 2)
                start = (((dp * 8 + z) * 2 + yl) * 2 + core) * 20
                order[at : at + 20] = np.arange(start, start + 20)
                at += 20
    return order.reshape(NX, 1, W)


def dot(a, b):
    return lax.dot_general(a, b, (((1,), (0,)), ((), ())), preferred_element_type=F32)


def dot_nt(a, b):
    return lax.dot_general(a, b, (((1,), (1,)), ((), ())), preferred_element_type=F32)


def call(kernel, out_shape, flops=0, grid_spec=None, limit=LIMIT, **kw):
    params = pltpu.CompilerParams(vmem_limit_bytes=limit)
    cost = pl.CostEstimate(flops=flops, bytes_accessed=4_000_000, transcendentals=0)
    if grid_spec is not None:
        kw["grid_spec"] = grid_spec
    return pl.pallas_call(kernel, out_shape=out_shape, compiler_params=params, cost_estimate=cost, **kw)


def to_chunks(rows):
    width = rows.shape[-1]
    half = rows.shape[0] // 2
    low = rows[:half].reshape(-1, PT, width)
    high = rows[half:].reshape(-1, PT, width)
    return jnp.concatenate([low, high], axis=1).astype(BF)


def one_hot(feat, among):
    places = lax.broadcasted_iota(jnp.int32, (among, W), 0)
    return jnp.where(places == feat, 1.0, 0.0).astype(BF)


def pick_kernel(x_ref, order_ref, go_hbm, n_hbm, out_hbm, rows_s, out_s, sems, out_sems):
    part = NT * PT // STEPS
    first = lax.rem(x_ref[0], 2) * (D // 2)
    fetches = [
        [
            pltpu.make_async_copy(
                hbm.at[f, pl.ds(i * part, part), pl.ds(pl.multiple_of(first, LANES), D // 2)],
                rows_s.at[at, i, f],
                sems.at[(at * STEPS + i) * FR + f],
            )
            for at, hbm in enumerate((go_hbm, n_hbm))
            for f in range(FR)
        ]
        for i in range(STEPS)
    ]
    for group in fetches:
        for fetch in group:
            fetch.start()
    pick = one_hot(order_ref[x_ref[0]] - first, D // 2)
    chunks = NT // STEPS
    stores = []
    for i in range(STEPS):
        for fetch in fetches[i]:
            fetch.wait()
        for at in range(2):
            rows = dot(rows_s[at, i].reshape(FR * part, D // 2), pick)
            out_s[i * chunks : (i + 1) * chunks, :, at * W : (at + 1) * W] = to_chunks(rows)
        own = pl.ds(i * chunks, chunks)
        stores.append(pltpu.make_async_copy(out_s.at[own], out_hbm.at[own], out_sems.at[i]))
        stores[-1].start()
    for store in stores:
        store.wait()


def pick(x, order, grad_output, normed):
    hbm = pl.BlockSpec(memory_space=pl.ANY)
    shape = (NT, 2 * PT, 2 * W)
    return call(
        pick_kernel,
        jax.ShapeDtypeStruct(shape, BF),
        850_000_000,
        limit=60 * 1024 * 1024,
        in_specs=[
            pl.BlockSpec(memory_space=pltpu.SMEM),
            pl.BlockSpec(memory_space=pltpu.VMEM),
            hbm,
            hbm,
        ],
        out_specs=hbm,
        scratch_shapes=[
            pltpu.VMEM((2, STEPS, FR, NT * PT // STEPS, D // 2), BF),
            pltpu.VMEM(shape, BF),
            pltpu.SemaphoreType.DMA((2 * STEPS * FR,)),
            pltpu.SemaphoreType.DMA((STEPS,)),
        ],
    )(x, order, grad_output, normed)


def pack_kernel(q_ref, k_ref, v_ref, out_ref):
    packed = [
        ref[...].reshape(FR * W, NT * PT).astype(F32).T.reshape(NT, PT, FR * W) for ref in (q_ref, k_ref, v_ref)
    ]
    out_ref[...] = jnp.concatenate(packed, axis=1).astype(BF)


def reorder_kernel(feat_ref, w_ref, out_ref):
    for at in range(NX):
        out_ref[at] = dot(w_ref[...], one_hot(feat_ref[at], D)).astype(BF)


def place(p, f):
    return (p // 4) * BLOCK + f * (BLOCK // 2) + (p % 4) * NT


def attend_kernel(x_ref, qkv_ref, gon_ref, wout_ref, wqkv_hbm, grads_ref, *rest):
    norm_refs, (wide_s, rows_s, v_s, qkvg_t, g_t, norm_s, go_s, wqkv_s, sems) = rest[:NX], rest[NX:]
    copies = [
        pltpu.make_async_copy(gon_ref.at[at, :, :, pl.ds(0, GO)], go_s.at[at], sems.at[at]) for at in range(NX)
    ]
    copies.append(pltpu.make_async_copy(wqkv_hbm, wqkv_s, sems.at[NX]))
    for copy in copies:
        copy.start()
    half = BLOCK // 2
    values = qkv_ref[...].astype(F32)
    for a in range(3):
        own = values[:, a * PT : (a + 1) * PT, :].reshape(NT * PT, FR * W)
        for t in range(HALF_TILES):
            wide_s[t, : NT * PT, :] = own[:, t * LANES : (t + 1) * LANES]
        for p in range(PT):
            for t in range(HALF_TILES):
                rows_s[p * NT : (p + 1) * NT, t * LANES : (t + 1) * LANES] = wide_s[t, pl.ds(p, NT, stride=PT), :]
        rows = rows_s[...]
        if a > 0:
            v_s[a - 1] = rows.astype(BF)
        turned = rows.T.astype(BF)
        for b in range(TOK // BLOCK):
            for f in range(FR):
                start = b * BLOCK + f * half
                qkvg_t[a * W : (a + 1) * W, start : start + half] = turned[
                    f * W : (f + 1) * W, b * half : (b + 1) * half
                ]
    acc = jnp.zeros((TOK, W), F32)
    for at in range(NX):
        copies[at].wait()
        acc = acc + dot_nt(go_s[at].reshape(TOK, GO)[:, :W], wout_ref[at])
    wide_s[0] = acc[:, :LANES]
    wide_s[1] = acc[:, LANES : 2 * LANES]
    wide_s[2, :, : W - 2 * LANES] = acc[:, 2 * LANES :]
    for p in range(PT):
        for f in range(FR):
            at = place(p, f)
            for t in range(3):
                wide = min(LANES, W - t * LANES)
                piece = wide_s[t, pl.ds(f * PT + p, NT, stride=FR * PT), :]
                g_t[at : at + NT, t * LANES : t * LANES + wide] = piece[:, :wide]
    qkvg_t[3 * W :, :] = g_t[:TOK, :W].T.astype(BF)
    row_patch = lax.broadcasted_iota(jnp.int32, (BLOCK, BLOCK), 0) // NT % 4
    col_patch = lax.broadcasted_iota(jnp.int32, (BLOCK, BLOCK), 1) // NT % 4
    same = row_patch == col_patch
    for b in range(TOK // BLOCK):
        cols = slice(b * BLOCK, (b + 1) * BLOCK)
        own = slice(b * half, (b + 1) * half)
        for h in range(HEADS):
            heads = [slice(i * W + h * HS, i * W + (h + 1) * HS) for i in range(4)]
            q_t, k_t, v_t, ga_t = [qkvg_t[head, cols] for head in heads]
            k_rows, v_rows = [
                jnp.concatenate([v_s[i, own, heads[f]] for f in range(FR)], axis=0) for i in range(2)
            ]
            scores = dot(k_rows, q_t) * TEMPER
            scores = jnp.where(same, scores, -jnp.inf)
            powers = jnp.exp(scores - jnp.max(scores, axis=0, keepdims=True))
            probs = powers * (1.0 / jnp.sum(powers, axis=0, keepdims=True))
            weights = probs.astype(BF)
            g_t[heads[3], cols] = dot(v_t, weights)
            grad_probs = dot(v_rows, ga_t)
            delta = jnp.sum(probs * grad_probs, axis=0, keepdims=True)
            grad_scores = (probs * (grad_probs - delta)).astype(BF)
            g_t[heads[0], cols] = dot(k_t, grad_scores) * TEMPER
            g_t[heads[1], cols] = dot_nt(q_t, grad_scores) * TEMPER
            g_t[heads[2], cols] = dot_nt(ga_t, weights)
    for t in range(TILES):
        tile = g_t[t * LANES : (t + 1) * LANES, :].T
        for p in range(PT):
            for f in range(FR):
                at = place(p, f)
                wide_s[t, pl.ds(f * PT + p, NT, stride=FR * PT), :] = tile[at : at + NT]
    for t in range(TILES):
        grads_ref[:, t * LANES : (t + 1) * LANES] = wide_s[t].astype(BF)
    copies[NX].wait()
    norm = dot(grads_ref[:, : 3 * W], wqkv_s[...])
    for at in range(NX):
        part = norm[:, at * W : (at + 1) * W].reshape(NT, 2 * PT, W)
        slot = lax.rem(at + NX - x_ref[0], NX)
        for f in range(FR):
            norm_s[slot, :, f * W : (f + 1) * W] = part[:, f * PT : (f + 1) * PT, :].reshape(NT * PT, W).astype(BF)
    for at in range(NX):
        norm_refs[at][...] = norm_s[at]


def attend(x, qkv, gon, w_ordered, w_qkv):
    scalar = pl.BlockSpec(memory_space=pltpu.SMEM)
    whole = pl.BlockSpec(memory_space=pltpu.VMEM)
    hbm = pl.BlockSpec(memory_space=pl.ANY)
    return call(
        attend_kernel,
        (jax.ShapeDtypeStruct((TOK, 4 * W), BF),) + (jax.ShapeDtypeStruct((TOK // 2, 2 * W), BF),) * NX,
        5_000_000_000,
        in_specs=[scalar, whole, hbm, whole, hbm],
        scratch_shapes=[
            pltpu.VMEM((TILES, TOK, LANES), F32),
            pltpu.VMEM((NT * PT, FR * W), F32),
            pltpu.VMEM((2, NT * PT, FR * W), BF),
            pltpu.VMEM((4 * W, TOK), BF),
            pltpu.VMEM((4 * W, TOK), F32),
            pltpu.VMEM((NX, TOK // 2, 2 * W), BF),
            pltpu.VMEM((NX, NT, 2 * PT, GO), BF),
            pltpu.VMEM((3 * W, D), BF),
            pltpu.SemaphoreType.DMA((NX + 1,)),
        ],
    )(x, qkv, gon, w_ordered, w_qkv)


def weight_kernel(half_ref, gon_ref, grads_ref, *refs):
    del half_ref
    out_ref = refs[-1]
    gon_t = gon_ref[0].reshape(TOK, 2 * W).astype(F32).T.astype(BF)
    for rows, cols in ((slice(W, 2 * W), slice(0, 3 * W)), (slice(0, W), slice(3 * W, 4 * W))):
        total = dot(gon_t[rows], grads_ref[:, cols])
        if len(refs) == 2:
            total = total + refs[0][:, cols].astype(F32)
        out_ref[:, cols] = total.astype(BF)


def weight_half(half, gon, grads, *got):
    block = pl.BlockSpec((W, 4 * W), lambda j, half: (j, 0))
    spec = pltpu.PrefetchScalarGridSpec(
        num_scalar_prefetch=1,
        grid=(2,),
        in_specs=[
            pl.BlockSpec((1, NT, 2 * PT, 2 * W), lambda j, half: (half[0] * 2 + j, 0, 0, 0)),
            pl.BlockSpec((TOK, 4 * W), lambda j, half: (0, 0)),
        ]
        + [block] * len(got),
        out_specs=block,
    )
    shape = jax.ShapeDtypeStruct((2 * W, 4 * W), BF)
    return call(weight_kernel, shape, 4_000_000_000, spec, 20 * 1024 * 1024)(half, gon, grads, *got)


def add_kernel(*refs):
    total = refs[0][...].astype(F32)
    for ref in refs[1:-1]:
        total = total + ref[...].astype(F32)
    refs[-1][...] = total.astype(BF)


def spread_kernel(x_ref, *refs):
    out_ref = refs[-1]
    for at in range(NX):
        for k in range(NX):

            @pl.when(lax.rem(x_ref[0] + NX - k, NX) == at)
            def _(at=at, k=k):
                for f in range(FR):
                    out_ref[f, :, at * W : (at + 1) * W] = refs[k][:, f * W : (f + 1) * W]


def regroup_kernel(in_ref, out_ref):
    rows = in_ref[...].astype(F32)
    for at in range(8):
        out_ref[at] = rows[at * 20 : (at + 1) * 20].astype(BF)


def total_kernel(in_ref, qkv_ref, out_ref):
    total = in_ref[0].astype(F32)
    for at in range(1, 8):
        total = total + in_ref[at].astype(F32)
    for i in range(3):
        qkv_ref[i] = total[:, i * W : (i + 1) * W]
    out_ref[...] = total[:, 3 * W :]


def shift(array, k):
    return lax.ppermute(array, "x", [(i, (i + k) % NX) for i in range(NX)])


def on_device(queries, key_vectors, value_vectors, normed, grad_output, w_qkv, w_out):
    order = jnp.asarray(feature_order())
    x = lax.axis_index("x")
    core = lax.axis_index("core")
    scalar = pl.BlockSpec(memory_space=pltpu.SMEM)
    whole = pl.BlockSpec(memory_space=pltpu.VMEM)
    gon = pick(x.reshape(1), order, grad_output[0], normed[0])
    gon = lax.all_to_all(gon, TM, 0, 0, tiled=True)
    gon = lax.all_gather(gon, "x", axis=0)
    qkv = call(pack_kernel, jax.ShapeDtypeStruct((NT, 3 * PT, FR * W), BF), 30_000_000_000)(
        *[jnp.swapaxes(item[0], 1, 2) for item in (queries, key_vectors, value_vectors)]
    )
    qkv = lax.all_to_all(qkv, TM, 0, 0, tiled=True)
    w_ordered = call(reorder_kernel, jax.ShapeDtypeStruct((NX, W, W), BF), 1_000_000_000)(order, w_out)
    grads, *parts = attend(x.reshape(1), qkv, gon, w_ordered, jnp.swapaxes(w_qkv, 1, 2).reshape(3 * W, D))

    moved = [parts[0]] + [shift(parts[k], k) for k in range(1, NX)]
    sent = weight_half((1 - core).reshape(1), gon, grads)
    got = lax.ppermute(sent, "core", [(0, 1), (1, 0)])
    both = weight_half(core.reshape(1), gon, grads, got).reshape(4, D // 8, 4 * W)
    quarter = lax.psum_scatter(both, Y, scatter_dimension=0, tiled=True)

    own_norm = call(add_kernel, jax.ShapeDtypeStruct((TOK // 2, 2 * W), BF), 40_000_000_000)(*moved)
    own_norm = lax.all_to_all(own_norm.reshape(NT, PT, 2 * W), TM, 0, 0, tiled=True).reshape(TOK // 2, 2 * W)
    all_norm = [own_norm] + [shift(own_norm, k) for k in range(1, NX)]
    grad_normed = call(
        spread_kernel,
        jax.ShapeDtypeStruct((FR, TOK // 2, D), BF),
        40_000_000_000,
        in_specs=[scalar] + [whole] * NX,
    )(x.reshape(1), *all_norm)

    pieces = call(regroup_kernel, jax.ShapeDtypeStruct((8, 20, 4 * W), BF), limit=60 * 1024 * 1024)(quarter.reshape(D // 8, 4 * W))
    pieces = lax.all_to_all(pieces, "z", 0, 0, tiled=True)
    grad_qkv, grad_out = call(
        total_kernel, (jax.ShapeDtypeStruct((3, 20, W), F32), jax.ShapeDtypeStruct((20, W), F32))
    )(pieces)
    return (grad_normed[None], grad_qkv, grad_out.T)


def solution(mesh):
    own = Mesh(mesh.devices.reshape(2, 8, 2, 2, 4), ("dp", "z", "yl", "core", "x"))
    in_specs = (
        P("dp", TM, None, "x"),
        P("dp", TM, None, "x"),
        P("dp", TM, None, "x"),
        P("dp", TM, None, None),
        P("dp", TM, None, None),
        P(None, None, "x"),
        P("x", None),
    )
    out_specs = (
        P("dp", TM, None, None),
        P(None, ("dp",) + TM, "x"),
        P("x", ("dp",) + TM),
    )
    return jax.shard_map(on_device, mesh=own, in_specs=in_specs, out_specs=out_specs, check_vma=False)
```

```python
import functools

import jax
import jax.numpy as jnp
import numpy as np
from jax import lax
from jax.experimental import pallas as pl
from jax.experimental.pallas import tpu as pltpu
from jax.sharding import Mesh
from jax.sharding import PartitionSpec as P

HS = 80
HEADS = 4
W = HEADS * HS
D = 1280
NX = 4
NT = 32
FR = 2
PT = 8
TOK = 512
FRAMES = 64
LANES = 128
STEPS = 2
GO = 384
TILES = 4 * W // LANES
HALF_TILES = 5
BLOCK = 256
TEMPER = HS ** (-0.5)
TM = ("z", "yl", "core")
Y = ("dp", "yl")
BF = jnp.bfloat16
F32 = jnp.float32
LIMIT = 48 * 1024 * 1024


def feature_order():
    order = np.zeros(D, np.int32)
    at = 0
    for core in range(2):
        for y in range(4):
            for z in range(8):
                dp, yl = divmod(y, 2)
                start = (((dp * 8 + z) * 2 + yl) * 2 + core) * 20
                order[at : at + 20] = np.arange(start, start + 20)
                at += 20
    return order.reshape(NX, 1, W)


def dot(a, b):
    return lax.dot_general(a, b, (((1,), (0,)), ((), ())), preferred_element_type=F32)


def dot_nt(a, b):
    return lax.dot_general(a, b, (((1,), (1,)), ((), ())), preferred_element_type=F32)


def call(kernel, out_shape, flops=0, grid_spec=None, limit=LIMIT, **kw):
    params = pltpu.CompilerParams(vmem_limit_bytes=limit)
    cost = pl.CostEstimate(flops=flops, bytes_accessed=4_000_000, transcendentals=0)
    if grid_spec is not None:
        kw["grid_spec"] = grid_spec
    return pl.pallas_call(kernel, out_shape=out_shape, compiler_params=params, cost_estimate=cost, **kw)


def to_chunks(rows):
    width = rows.shape[-1]
    half = rows.shape[0] // 2
    low = rows[:half].reshape(-1, PT, width)
    high = rows[half:].reshape(-1, PT, width)
    return jnp.concatenate([low, high], axis=1).astype(BF)


def one_hot(feat, among):
    places = lax.broadcasted_iota(jnp.int32, (among, W), 0)
    return jnp.where(places == feat, 1.0, 0.0).astype(BF)


def pick_kernel(x_ref, go_hbm, n_hbm, out_hbm, rows_s, out_s, sems, out_sems):
    part = NT * PT // STEPS
    first = lax.rem(x_ref[0], 2) * (D // 2)
    fetches = [
        [
            pltpu.make_async_copy(
                hbm.at[f, pl.ds(i * part, part), pl.ds(pl.multiple_of(first, LANES), D // 2)],
                rows_s.at[at, i, f],
                sems.at[(at * STEPS + i) * FR + f],
            )
            for at, hbm in enumerate((go_hbm, n_hbm))
            for f in range(FR)
        ]
        for i in range(STEPS)
    ]
    for group in fetches:
        for fetch in group:
            fetch.start()
    at = lax.broadcasted_iota(jnp.int32, (1, W), 1)
    low = (at >= W // 2).astype(jnp.int32)
    z = sum((at - low * (W // 2) >= 20 * k).astype(jnp.int32) for k in range(1, 8))
    start = z * 80 + low * 40 + lax.div(x_ref[0], 2) * 20
    pick = one_hot(start + at - low * (W // 2) - z * 20, D // 2)
    chunks = NT // STEPS
    stores = []
    for i in range(STEPS):
        for fetch in fetches[i]:
            fetch.wait()
        for at in range(2):
            rows = dot(rows_s[at, i].reshape(FR * part, D // 2), pick)
            out_s[i * chunks : (i + 1) * chunks, :, at * W : (at + 1) * W] = to_chunks(rows)
        own = pl.ds(i * chunks, chunks)
        stores.append(pltpu.make_async_copy(out_s.at[own], out_hbm.at[own], out_sems.at[i]))
        stores[-1].start()
    for store in stores:
        store.wait()


def pick(x, grad_output, normed):
    hbm = pl.BlockSpec(memory_space=pl.ANY)
    shape = (NT, 2 * PT, 2 * W)
    return call(
        pick_kernel,
        jax.ShapeDtypeStruct(shape, BF),
        850_000_000,
        limit=60 * 1024 * 1024,
        in_specs=[
            pl.BlockSpec(memory_space=pltpu.SMEM),
            hbm,
            hbm,
        ],
        out_specs=hbm,
        scratch_shapes=[
            pltpu.VMEM((2, STEPS, FR, NT * PT // STEPS, D // 2), BF),
            pltpu.VMEM(shape, BF),
            pltpu.SemaphoreType.DMA((2 * STEPS * FR,)),
            pltpu.SemaphoreType.DMA((STEPS,)),
        ],
    )(x, grad_output, normed)


def pack_kernel(q_ref, k_ref, v_ref, out_ref):
    packed = [
        ref[...].reshape(FR * W, NT * PT).astype(F32).T.reshape(NT, PT, FR * W) for ref in (q_ref, k_ref, v_ref)
    ]
    out_ref[...] = jnp.concatenate(packed, axis=1).astype(BF)


def reorder_kernel(feat_ref, w_ref, out_ref):
    for at in range(NX):
        out_ref[at] = dot(w_ref[...], one_hot(feat_ref[at], D)).astype(BF)


def place(p, f):
    return (p // 4) * BLOCK + f * (BLOCK // 2) + (p % 4) * NT


def attend_kernel(x_ref, qkv_ref, gon_ref, wout_ref, wqkv_hbm, grads_ref, *rest):
    norm_refs, (wide_s, rows_s, v_s, qkvg_t, g_t, norm_s, go_s, wqkv_s, sems) = rest[:NX], rest[NX:]
    copies = [
        pltpu.make_async_copy(gon_ref.at[at, :, :, pl.ds(0, GO)], go_s.at[at], sems.at[at]) for at in range(NX)
    ]
    copies.append(pltpu.make_async_copy(wqkv_hbm, wqkv_s, sems.at[NX]))
    for copy in copies:
        copy.start()
    half = BLOCK // 2
    values = qkv_ref[...].astype(F32)
    for a in range(3):
        own = values[:, a * PT : (a + 1) * PT, :].reshape(NT * PT, FR * W)
        for t in range(HALF_TILES):
            wide_s[t, : NT * PT, :] = own[:, t * LANES : (t + 1) * LANES]
        for p in range(PT):
            for t in range(HALF_TILES):
                rows_s[p * NT : (p + 1) * NT, t * LANES : (t + 1) * LANES] = wide_s[t, pl.ds(p, NT, stride=PT), :]
        rows = rows_s[...]
        if a > 0:
            v_s[a - 1] = rows.astype(BF)
        turned = rows.T.astype(BF)
        for b in range(TOK // BLOCK):
            for f in range(FR):
                start = b * BLOCK + f * half
                qkvg_t[a * W : (a + 1) * W, start : start + half] = turned[
                    f * W : (f + 1) * W, b * half : (b + 1) * half
                ]
    acc = jnp.zeros((TOK, W), F32)
    for at in range(NX):
        copies[at].wait()
        acc = acc + dot_nt(go_s[at].reshape(TOK, GO)[:, :W], wout_ref[at])
    wide_s[0] = acc[:, :LANES]
    wide_s[1] = acc[:, LANES : 2 * LANES]
    wide_s[2, :, : W - 2 * LANES] = acc[:, 2 * LANES :]
    for p in range(PT):
        for f in range(FR):
            at = place(p, f)
            for t in range(3):
                wide = min(LANES, W - t * LANES)
                piece = wide_s[t, pl.ds(f * PT + p, NT, stride=FR * PT), :]
                g_t[at : at + NT, t * LANES : t * LANES + wide] = piece[:, :wide]
    qkvg_t[3 * W :, :] = g_t[:TOK, :W].T.astype(BF)
    row_patch = lax.broadcasted_iota(jnp.int32, (BLOCK, BLOCK), 0) // NT % 4
    col_patch = lax.broadcasted_iota(jnp.int32, (BLOCK, BLOCK), 1) // NT % 4
    same = row_patch == col_patch
    for b in range(TOK // BLOCK):
        cols = slice(b * BLOCK, (b + 1) * BLOCK)
        own = slice(b * half, (b + 1) * half)
        for h in range(HEADS):
            heads = [slice(i * W + h * HS, i * W + (h + 1) * HS) for i in range(4)]
            q_t, k_t, v_t, ga_t = [qkvg_t[head, cols] for head in heads]
            k_rows, v_rows = [
                jnp.concatenate([v_s[i, own, heads[f]] for f in range(FR)], axis=0) for i in range(2)
            ]
            scores = dot(k_rows, q_t) * TEMPER
            scores = jnp.where(same, scores, -jnp.inf)
            powers = jnp.exp(scores - jnp.max(scores, axis=0, keepdims=True))
            probs = powers * (1.0 / jnp.sum(powers, axis=0, keepdims=True))
            weights = probs.astype(BF)
            g_t[heads[3], cols] = dot(v_t, weights)
            grad_probs = dot(v_rows, ga_t)
            delta = jnp.sum(probs * grad_probs, axis=0, keepdims=True)
            grad_scores = (probs * (grad_probs - delta)).astype(BF)
            g_t[heads[0], cols] = dot(k_t, grad_scores) * TEMPER
            g_t[heads[1], cols] = dot_nt(q_t, grad_scores) * TEMPER
            g_t[heads[2], cols] = dot_nt(ga_t, weights)
    for t in range(TILES):
        tile = g_t[t * LANES : (t + 1) * LANES, :].T
        for p in range(PT):
            for f in range(FR):
                at = place(p, f)
                wide_s[t, pl.ds(f * PT + p, NT, stride=FR * PT), :] = tile[at : at + NT]
    for t in range(TILES):
        grads_ref[:, t * LANES : (t + 1) * LANES] = wide_s[t].astype(BF)
    copies[NX].wait()
    norm = dot(grads_ref[:, : 3 * W], wqkv_s[...])
    for at in range(NX):
        part = norm[:, at * W : (at + 1) * W].reshape(NT, 2 * PT, W)
        slot = lax.rem(at + NX - x_ref[0], NX)
        for f in range(FR):
            norm_s[slot, :, f * W : (f + 1) * W] = part[:, f * PT : (f + 1) * PT, :].reshape(NT * PT, W).astype(BF)
    for at in range(NX):
        norm_refs[at][...] = norm_s[at]


def attend(x, qkv, gon, w_ordered, w_qkv):
    scalar = pl.BlockSpec(memory_space=pltpu.SMEM)
    whole = pl.BlockSpec(memory_space=pltpu.VMEM)
    hbm = pl.BlockSpec(memory_space=pl.ANY)
    return call(
        attend_kernel,
        (jax.ShapeDtypeStruct((TOK, 4 * W), BF),) + (jax.ShapeDtypeStruct((TOK // 2, 2 * W), BF),) * NX,
        5_000_000_000,
        in_specs=[scalar, whole, hbm, whole, hbm],
        scratch_shapes=[
            pltpu.VMEM((TILES, TOK, LANES), F32),
            pltpu.VMEM((NT * PT, FR * W), F32),
            pltpu.VMEM((2, NT * PT, FR * W), BF),
            pltpu.VMEM((4 * W, TOK), BF),
            pltpu.VMEM((4 * W, TOK), F32),
            pltpu.VMEM((NX, TOK // 2, 2 * W), BF),
            pltpu.VMEM((NX, NT, 2 * PT, GO), BF),
            pltpu.VMEM((3 * W, D), BF),
            pltpu.SemaphoreType.DMA((NX + 1,)),
        ],
    )(x, qkv, gon, w_ordered, w_qkv)


def weight_kernel(half_ref, gon_ref, grads_ref, *refs):
    del half_ref
    out_ref = refs[-1]
    gon_t = gon_ref[0].reshape(TOK, 2 * W).astype(F32).T.astype(BF)
    for rows, cols in ((slice(W, 2 * W), slice(0, 3 * W)), (slice(0, W), slice(3 * W, 4 * W))):
        total = dot(gon_t[rows], grads_ref[:, cols])
        if len(refs) == 2:
            total = total + refs[0][:, cols].astype(F32)
        out_ref[:, cols] = total.astype(BF)


def weight_half(half, gon, grads, *got):
    block = pl.BlockSpec((W, 4 * W), lambda j, half: (j, 0))
    spec = pltpu.PrefetchScalarGridSpec(
        num_scalar_prefetch=1,
        grid=(2,),
        in_specs=[
            pl.BlockSpec((1, NT, 2 * PT, 2 * W), lambda j, half: (half[0] * 2 + j, 0, 0, 0)),
            pl.BlockSpec((TOK, 4 * W), lambda j, half: (0, 0)),
        ]
        + [block] * len(got),
        out_specs=block,
    )
    shape = jax.ShapeDtypeStruct((2 * W, 4 * W), BF)
    return call(weight_kernel, shape, 4_000_000_000, spec, 20 * 1024 * 1024)(half, gon, grads, *got)


def add_kernel(*refs):
    total = refs[0][...].astype(F32)
    for ref in refs[1:-1]:
        total = total + ref[...].astype(F32)
    refs[-1][...] = total.astype(BF)


def spread_kernel(x_ref, *refs):
    out_ref = refs[-1]
    for at in range(NX):
        for k in range(NX):

            @pl.when(lax.rem(x_ref[0] + NX - k, NX) == at)
            def _(at=at, k=k):
                for f in range(FR):
                    out_ref[f, :, at * W : (at + 1) * W] = refs[k][:, f * W : (f + 1) * W]


def regroup_kernel(in_ref, out_ref):
    rows = in_ref[...].astype(F32)
    for at in range(8):
        out_ref[at] = rows[at * 20 : (at + 1) * 20].astype(BF)


def total_kernel(in_ref, qkv_ref, out_ref):
    total = in_ref[0].astype(F32)
    for at in range(1, 8):
        total = total + in_ref[at].astype(F32)
    for i in range(3):
        qkv_ref[i] = total[:, i * W : (i + 1) * W]
    out_ref[...] = total[:, 3 * W :]


def shift(array, k):
    return lax.ppermute(array, "x", [(i, (i + k) % NX) for i in range(NX)])


def on_device(queries, key_vectors, value_vectors, normed, grad_output, w_qkv, w_out):
    order = jnp.asarray(feature_order())
    x = lax.axis_index("x")
    core = lax.axis_index("core")
    scalar = pl.BlockSpec(memory_space=pltpu.SMEM)
    whole = pl.BlockSpec(memory_space=pltpu.VMEM)
    gon = pick(x.reshape(1), grad_output[0], normed[0])
    gon = lax.all_to_all(gon, TM, 0, 0, tiled=True)
    gon = lax.all_gather(gon, "x", axis=0)
    qkv = call(pack_kernel, jax.ShapeDtypeStruct((NT, 3 * PT, FR * W), BF), 30_000_000_000)(
        *[jnp.swapaxes(item[0], 1, 2) for item in (queries, key_vectors, value_vectors)]
    )
    qkv = lax.all_to_all(qkv, TM, 0, 0, tiled=True)
    w_ordered = call(reorder_kernel, jax.ShapeDtypeStruct((NX, W, W), BF), 1_000_000_000)(order, w_out)
    grads, *parts = attend(x.reshape(1), qkv, gon, w_ordered, jnp.swapaxes(w_qkv, 1, 2).reshape(3 * W, D))

    moved = [parts[0]] + [shift(parts[k], k) for k in range(1, NX)]
    sent = weight_half((1 - core).reshape(1), gon, grads)
    got = lax.ppermute(sent, "core", [(0, 1), (1, 0)])
    both = weight_half(core.reshape(1), gon, grads, got).reshape(4, D // 8, 4 * W)
    quarter = lax.psum_scatter(both, Y, scatter_dimension=0, tiled=True)

    own_norm = call(add_kernel, jax.ShapeDtypeStruct((TOK // 2, 2 * W), BF), 40_000_000_000)(*moved)
    own_norm = lax.all_to_all(own_norm.reshape(NT, PT, 2 * W), TM, 0, 0, tiled=True).reshape(TOK // 2, 2 * W)
    all_norm = [own_norm] + [shift(own_norm, k) for k in range(1, NX)]
    grad_normed = call(
        spread_kernel,
        jax.ShapeDtypeStruct((FR, TOK // 2, D), BF),
        40_000_000_000,
        in_specs=[scalar] + [whole] * NX,
    )(x.reshape(1), *all_norm)

    pieces = call(regroup_kernel, jax.ShapeDtypeStruct((8, 20, 4 * W), BF), limit=60 * 1024 * 1024)(quarter.reshape(D // 8, 4 * W))
    pieces = lax.all_to_all(pieces, "z", 0, 0, tiled=True)
    grad_qkv, grad_out = call(
        total_kernel, (jax.ShapeDtypeStruct((3, 20, W), F32), jax.ShapeDtypeStruct((20, W), F32))
    )(pieces)
    return (grad_normed[None], grad_qkv, grad_out.T)


def solution(mesh):
    own = Mesh(mesh.devices.reshape(2, 8, 2, 2, 4), ("dp", "z", "yl", "core", "x"))
    in_specs = (
        P("dp", TM, None, "x"),
        P("dp", TM, None, "x"),
        P("dp", TM, None, "x"),
        P("dp", TM, None, None),
        P("dp", TM, None, None),
        P(None, None, "x"),
        P("x", None),
    )
    out_specs = (
        P("dp", TM, None, None),
        P(None, ("dp",) + TM, "x"),
        P("x", ("dp",) + TM),
    )
    return jax.shard_map(on_device, mesh=own, in_specs=in_specs, out_specs=out_specs, check_vma=False)
```

```python
import functools

import jax
import jax.numpy as jnp
import numpy as np
from jax import lax
from jax.experimental import pallas as pl
from jax.experimental.pallas import tpu as pltpu
from jax.sharding import Mesh
from jax.sharding import PartitionSpec as P

HS = 80
HEADS = 4
W = HEADS * HS
D = 1280
NX = 4
NT = 32
FR = 2
PT = 8
TOK = 512
FRAMES = 64
LANES = 128
STEPS = 2
GO = 384
TILES = 4 * W // LANES
HALF_TILES = 5
BLOCK = 256
TEMPER = HS ** (-0.5)
TM = ("z", "yl", "core")
Y = ("dp", "yl")
BF = jnp.bfloat16
F32 = jnp.float32
LIMIT = 48 * 1024 * 1024


def feature_order():
    order = np.zeros(D, np.int32)
    at = 0
    for core in range(2):
        for y in range(4):
            for z in range(8):
                dp, yl = divmod(y, 2)
                start = (((dp * 8 + z) * 2 + yl) * 2 + core) * 20
                order[at : at + 20] = np.arange(start, start + 20)
                at += 20
    return order.reshape(NX, 1, W)


def dot(a, b):
    return lax.dot_general(a, b, (((1,), (0,)), ((), ())), preferred_element_type=F32)


def dot_nt(a, b):
    return lax.dot_general(a, b, (((1,), (1,)), ((), ())), preferred_element_type=F32)


def call(kernel, out_shape, flops=0, grid_spec=None, limit=LIMIT, **kw):
    params = pltpu.CompilerParams(vmem_limit_bytes=limit)
    cost = pl.CostEstimate(flops=flops, bytes_accessed=4_000_000, transcendentals=0)
    if grid_spec is not None:
        kw["grid_spec"] = grid_spec
    return pl.pallas_call(kernel, out_shape=out_shape, compiler_params=params, cost_estimate=cost, **kw)


def to_chunks(rows):
    width = rows.shape[-1]
    half = rows.shape[0] // 2
    low = rows[:half].reshape(-1, PT, width)
    high = rows[half:].reshape(-1, PT, width)
    return jnp.concatenate([low, high], axis=1).astype(BF)


def one_hot(feat, among):
    places = lax.broadcasted_iota(jnp.int32, (among, W), 0)
    return jnp.where(places == feat, 1.0, 0.0).astype(BF)


def pick_kernel(x_ref, go_hbm, n_hbm, out_hbm, rows_s, out_s, sems, out_sems):
    part = NT * PT // STEPS
    first = lax.rem(x_ref[0], 2) * (D // 2)
    fetches = [
        [
            pltpu.make_async_copy(
                hbm.at[f, pl.ds(i * part, part), pl.ds(pl.multiple_of(first, LANES), D // 2)],
                rows_s.at[at, i, f],
                sems.at[(at * STEPS + i) * FR + f],
            )
            for at, hbm in enumerate((go_hbm, n_hbm))
            for f in range(FR)
        ]
        for i in range(STEPS)
    ]
    for group in fetches:
        for fetch in group:
            fetch.start()
    at = lax.broadcasted_iota(jnp.int32, (1, W), 1)
    low = (at >= W // 2).astype(jnp.int32)
    z = sum((at - low * (W // 2) >= 20 * k).astype(jnp.int32) for k in range(1, 8))
    start = z * 80 + low * 40 + lax.div(x_ref[0], 2) * 20
    pick = one_hot(start + at - low * (W // 2) - z * 20, D // 2)
    chunks = NT // STEPS
    stores = []
    for i in range(STEPS):
        for fetch in fetches[i]:
            fetch.wait()
        for at in range(2):
            rows = dot(rows_s[at, i].reshape(FR * part, D // 2), pick)
            out_s[i * chunks : (i + 1) * chunks, :, at * W : (at + 1) * W] = to_chunks(rows)
        own = pl.ds(i * chunks, chunks)
        stores.append(pltpu.make_async_copy(out_s.at[own], out_hbm.at[own], out_sems.at[i]))
        stores[-1].start()
    for store in stores:
        store.wait()


def pick(x, grad_output, normed):
    hbm = pl.BlockSpec(memory_space=pl.ANY)
    shape = (NT, 2 * PT, 2 * W)
    return call(
        pick_kernel,
        jax.ShapeDtypeStruct(shape, BF),
        850_000_000,
        limit=60 * 1024 * 1024,
        in_specs=[
            pl.BlockSpec(memory_space=pltpu.SMEM),
            hbm,
            hbm,
        ],
        out_specs=hbm,
        scratch_shapes=[
            pltpu.VMEM((2, STEPS, FR, NT * PT // STEPS, D // 2), BF),
            pltpu.VMEM(shape, BF),
            pltpu.SemaphoreType.DMA((2 * STEPS * FR,)),
            pltpu.SemaphoreType.DMA((STEPS,)),
        ],
    )(x, grad_output, normed)


def pack_kernel(q_ref, k_ref, v_ref, out_ref):
    packed = [
        ref[...].reshape(FR * W, NT * PT).astype(F32).T.reshape(NT, PT, FR * W) for ref in (q_ref, k_ref, v_ref)
    ]
    out_ref[...] = jnp.concatenate(packed, axis=1).astype(BF)


def reorder_kernel(feat_ref, w_ref, out_ref):
    for at in range(NX):
        out_ref[at] = dot(w_ref[...], one_hot(feat_ref[at], D)).astype(BF)


def place(p, f):
    return (p // 4) * BLOCK + f * (BLOCK // 2) + (p % 4) * NT


def attend_kernel(x_ref, qkv_ref, gon_ref, wout_ref, wqkv_hbm, grads_ref, *rest):
    norm_refs, (wide_s, rows_s, v_s, qkvg_t, g_t, norm_s, go_s, wqkv_s, sems) = rest[:NX], rest[NX:]
    copies = [
        pltpu.make_async_copy(gon_ref.at[at, :, :, pl.ds(0, GO)], go_s.at[at], sems.at[at]) for at in range(NX)
    ]
    copies.append(pltpu.make_async_copy(wqkv_hbm, wqkv_s, sems.at[NX]))
    for copy in copies:
        copy.start()
    half = BLOCK // 2
    values = qkv_ref[...].astype(F32)
    for a in range(3):
        own = values[:, a * PT : (a + 1) * PT, :].reshape(NT * PT, FR * W)
        for t in range(HALF_TILES):
            wide_s[t, : NT * PT, :] = own[:, t * LANES : (t + 1) * LANES]
        for p in range(PT):
            for t in range(HALF_TILES):
                rows_s[p * NT : (p + 1) * NT, t * LANES : (t + 1) * LANES] = wide_s[t, pl.ds(p, NT, stride=PT), :]
        rows = rows_s[...]
        if a > 0:
            v_s[a - 1] = rows.astype(BF)
        turned = rows.T.astype(BF)
        for b in range(TOK // BLOCK):
            for f in range(FR):
                start = b * BLOCK + f * half
                qkvg_t[a * W : (a + 1) * W, start : start + half] = turned[
                    f * W : (f + 1) * W, b * half : (b + 1) * half
                ]
    acc = jnp.zeros((TOK, W), F32)
    for at in range(NX):
        copies[at].wait()
        acc = acc + dot_nt(go_s[at].reshape(TOK, GO)[:, :W], wout_ref[at])
    wide_s[0] = acc[:, :LANES]
    wide_s[1] = acc[:, LANES : 2 * LANES]
    wide_s[2, :, : W - 2 * LANES] = acc[:, 2 * LANES :]
    for p in range(PT):
        for f in range(FR):
            at = place(p, f)
            for t in range(3):
                wide = min(LANES, W - t * LANES)
                piece = wide_s[t, pl.ds(f * PT + p, NT, stride=FR * PT), :]
                g_t[at : at + NT, t * LANES : t * LANES + wide] = piece[:, :wide]
    qkvg_t[3 * W :, :] = g_t[:TOK, :W].T.astype(BF)
    row_patch = lax.broadcasted_iota(jnp.int32, (BLOCK, BLOCK), 0) // NT % 4
    col_patch = lax.broadcasted_iota(jnp.int32, (BLOCK, BLOCK), 1) // NT % 4
    same = row_patch == col_patch
    for b in range(TOK // BLOCK):
        cols = slice(b * BLOCK, (b + 1) * BLOCK)
        own = slice(b * half, (b + 1) * half)
        for h in range(HEADS):
            heads = [slice(i * W + h * HS, i * W + (h + 1) * HS) for i in range(4)]
            q_t, k_t, v_t, ga_t = [qkvg_t[head, cols] for head in heads]
            k_rows, v_rows = [
                jnp.concatenate([v_s[i, own, heads[f]] for f in range(FR)], axis=0) for i in range(2)
            ]
            scores = dot(k_rows, q_t) * TEMPER
            scores = jnp.where(same, scores, -jnp.inf)
            powers = jnp.exp(scores - jnp.max(scores, axis=0, keepdims=True))
            probs = powers * (1.0 / jnp.sum(powers, axis=0, keepdims=True))
            weights = probs.astype(BF)
            g_t[heads[3], cols] = dot(v_t, weights)
            grad_probs = dot(v_rows, ga_t)
            delta = jnp.sum(probs * grad_probs, axis=0, keepdims=True)
            grad_scores = (probs * (grad_probs - delta)).astype(BF)
            g_t[heads[0], cols] = dot(k_t, grad_scores) * TEMPER
            g_t[heads[1], cols] = dot_nt(q_t, grad_scores) * TEMPER
            g_t[heads[2], cols] = dot_nt(ga_t, weights)
    for t in range(TILES):
        tile = g_t[t * LANES : (t + 1) * LANES, :].T
        for p in range(PT):
            for f in range(FR):
                at = place(p, f)
                wide_s[t, pl.ds(f * PT + p, NT, stride=FR * PT), :] = tile[at : at + NT]
    for t in range(TILES):
        grads_ref[:, t * LANES : (t + 1) * LANES] = wide_s[t].astype(BF)
    copies[NX].wait()
    norm = dot(grads_ref[:, : 3 * W], wqkv_s[...])
    for at in range(NX):
        part = norm[:, at * W : (at + 1) * W].reshape(NT, 2 * PT, W)
        slot = lax.rem(at + NX - x_ref[0], NX)
        for f in range(FR):
            norm_s[slot, :, f * W : (f + 1) * W] = part[:, f * PT : (f + 1) * PT, :].reshape(NT * PT, W).astype(BF)
    for at in range(NX):
        norm_refs[at][...] = norm_s[at]


def attend(x, qkv, gon, w_ordered, w_qkv):
    scalar = pl.BlockSpec(memory_space=pltpu.SMEM)
    whole = pl.BlockSpec(memory_space=pltpu.VMEM)
    hbm = pl.BlockSpec(memory_space=pl.ANY)
    return call(
        attend_kernel,
        (jax.ShapeDtypeStruct((TOK, 4 * W), BF),) + (jax.ShapeDtypeStruct((TOK // 2, 2 * W), BF),) * NX,
        5_000_000_000,
        in_specs=[scalar, whole, hbm, whole, hbm],
        scratch_shapes=[
            pltpu.VMEM((TILES, TOK, LANES), F32),
            pltpu.VMEM((NT * PT, FR * W), F32),
            pltpu.VMEM((2, NT * PT, FR * W), BF),
            pltpu.VMEM((4 * W, TOK), BF),
            pltpu.VMEM((4 * W, TOK), F32),
            pltpu.VMEM((NX, TOK // 2, 2 * W), BF),
            pltpu.VMEM((NX, NT, 2 * PT, GO), BF),
            pltpu.VMEM((3 * W, D), BF),
            pltpu.SemaphoreType.DMA((NX + 1,)),
        ],
    )(x, qkv, gon, w_ordered, w_qkv)


def weight_kernel(half_ref, gon_ref, grads_ref, *refs):
    del half_ref
    out_ref = refs[-1]
    gon_t = gon_ref[0].reshape(TOK, 2 * W).astype(F32).T.astype(BF)
    for rows, cols in ((slice(W, 2 * W), slice(0, 3 * W)), (slice(0, W), slice(3 * W, 4 * W))):
        total = dot(gon_t[rows], grads_ref[:, cols])
        if len(refs) == 2:
            total = total + refs[0][:, cols].astype(F32)
        out_ref[:, cols] = total.astype(BF)


def weight_half(half, gon, grads, *got):
    block = pl.BlockSpec((W, 4 * W), lambda j, half: (j, 0))
    spec = pltpu.PrefetchScalarGridSpec(
        num_scalar_prefetch=1,
        grid=(2,),
        in_specs=[
            pl.BlockSpec((1, NT, 2 * PT, 2 * W), lambda j, half: (half[0] * 2 + j, 0, 0, 0)),
            pl.BlockSpec((TOK, 4 * W), lambda j, half: (0, 0)),
        ]
        + [block] * len(got),
        out_specs=block,
    )
    shape = jax.ShapeDtypeStruct((2 * W, 4 * W), BF)
    return call(weight_kernel, shape, 4_000_000_000, spec, 20 * 1024 * 1024)(half, gon, grads, *got)


def add_kernel(*refs):
    total = refs[0][...].astype(F32)
    for ref in refs[1:-1]:
        total = total + ref[...].astype(F32)
    refs[-1][...] = total.astype(BF)


def spread_kernel(x_ref, *refs):
    out_ref = refs[-1]
    for at in range(NX):
        for k in range(NX):

            @pl.when(lax.rem(x_ref[0] + NX - k, NX) == at)
            def _(at=at, k=k):
                for f in range(FR):
                    out_ref[f, :, at * W : (at + 1) * W] = refs[k][:, f * W : (f + 1) * W]


def regroup_kernel(in_ref, out_ref):
    rows = in_ref[...].astype(F32)
    for at in range(8):
        out_ref[at] = rows[at * 20 : (at + 1) * 20].astype(BF)


def total_kernel(in_ref, qkv_ref, out_ref):
    total = in_ref[0].astype(F32)
    for at in range(1, 8):
        total = total + in_ref[at].astype(F32)
    for i in range(3):
        qkv_ref[i] = total[:, i * W : (i + 1) * W]
    out_ref[...] = total[:, 3 * W :]


def shift(array, k):
    return lax.ppermute(array, "x", [(i, (i + k) % NX) for i in range(NX)])


def on_device(queries, key_vectors, value_vectors, normed, grad_output, w_qkv, w_out):
    order = jnp.asarray(feature_order())
    x = lax.axis_index("x")
    core = lax.axis_index("core")
    scalar = pl.BlockSpec(memory_space=pltpu.SMEM)
    whole = pl.BlockSpec(memory_space=pltpu.VMEM)
    gon = pick(x.reshape(1), grad_output[0], normed[0])
    gon = lax.all_to_all(gon, TM, 0, 0, tiled=True)
    gon = lax.all_gather(gon.reshape(TOK, 2 * W), "x", axis=0, tiled=True).reshape(NX, NT, 2 * PT, 2 * W)
    qkv = call(pack_kernel, jax.ShapeDtypeStruct((NT, 3 * PT, FR * W), BF), 30_000_000_000)(
        *[jnp.swapaxes(item[0], 1, 2) for item in (queries, key_vectors, value_vectors)]
    )
    qkv = lax.all_to_all(qkv, TM, 0, 0, tiled=True)
    w_ordered = call(reorder_kernel, jax.ShapeDtypeStruct((NX, W, W), BF), 1_000_000_000)(order, w_out)
    grads, *parts = attend(x.reshape(1), qkv, gon, w_ordered, jnp.swapaxes(w_qkv, 1, 2).reshape(3 * W, D))

    moved = [parts[0]] + [shift(parts[k], k) for k in range(1, NX)]
    sent = weight_half((1 - core).reshape(1), gon, grads)
    got = lax.ppermute(sent, "core", [(0, 1), (1, 0)])
    both = weight_half(core.reshape(1), gon, grads, got).reshape(4, D // 8, 4 * W)
    quarter = lax.psum_scatter(both, Y, scatter_dimension=0, tiled=True)

    own_norm = call(add_kernel, jax.ShapeDtypeStruct((TOK // 2, 2 * W), BF), 40_000_000_000)(*moved)
    own_norm = lax.all_to_all(own_norm.reshape(NT, PT, 2 * W), TM, 0, 0, tiled=True).reshape(TOK // 2, 2 * W)
    all_norm = [own_norm] + [shift(own_norm, k) for k in range(1, NX)]
    grad_normed = call(
        spread_kernel,
        jax.ShapeDtypeStruct((FR, TOK // 2, D), BF),
        40_000_000_000,
        in_specs=[scalar] + [whole] * NX,
    )(x.reshape(1), *all_norm)

    pieces = call(regroup_kernel, jax.ShapeDtypeStruct((8, 20, 4 * W), BF), limit=60 * 1024 * 1024)(quarter.reshape(D // 8, 4 * W))
    pieces = lax.all_to_all(pieces, "z", 0, 0, tiled=True)
    grad_qkv, grad_out = call(
        total_kernel, (jax.ShapeDtypeStruct((3, 20, W), F32), jax.ShapeDtypeStruct((20, W), F32))
    )(pieces)
    return (grad_normed[None], grad_qkv, grad_out.T)


def solution(mesh):
    own = Mesh(mesh.devices.reshape(2, 8, 2, 2, 4), ("dp", "z", "yl", "core", "x"))
    in_specs = (
        P("dp", TM, None, "x"),
        P("dp", TM, None, "x"),
        P("dp", TM, None, "x"),
        P("dp", TM, None, None),
        P("dp", TM, None, None),
        P(None, None, "x"),
        P("x", None),
    )
    out_specs = (
        P("dp", TM, None, None),
        P(None, ("dp",) + TM, "x"),
        P("x", ("dp",) + TM),
    )
    return jax.shard_map(on_device, mesh=own, in_specs=in_specs, out_specs=out_specs, check_vma=False)
```

```python
import functools

import jax
import jax.numpy as jnp
import numpy as np
from jax import lax
from jax.experimental import pallas as pl
from jax.experimental.pallas import tpu as pltpu
from jax.sharding import Mesh
from jax.sharding import PartitionSpec as P

HS = 80
HEADS = 4
W = HEADS * HS
D = 1280
NX = 4
NT = 32
FR = 2
PT = 8
TOK = 512
FRAMES = 64
LANES = 128
STEPS = 2
GO = 384
TILES = 4 * W // LANES
HALF_TILES = 5
BLOCK = 256
TEMPER = HS ** (-0.5)
TM = ("z", "yl", "core")
Y = ("dp", "yl")
BF = jnp.bfloat16
F32 = jnp.float32
LIMIT = 48 * 1024 * 1024


def feature_order():
    order = np.zeros(D, np.int32)
    at = 0
    for core in range(2):
        for y in range(4):
            for z in range(8):
                dp, yl = divmod(y, 2)
                start = (((dp * 8 + z) * 2 + yl) * 2 + core) * 20
                order[at : at + 20] = np.arange(start, start + 20)
                at += 20
    return order.reshape(NX, 1, W)


def dot(a, b):
    return lax.dot_general(a, b, (((1,), (0,)), ((), ())), preferred_element_type=F32)


def dot_nt(a, b):
    return lax.dot_general(a, b, (((1,), (1,)), ((), ())), preferred_element_type=F32)


def call(kernel, out_shape, flops=0, grid_spec=None, limit=LIMIT, **kw):
    params = pltpu.CompilerParams(vmem_limit_bytes=limit)
    cost = pl.CostEstimate(flops=flops, bytes_accessed=4_000_000, transcendentals=0)
    if grid_spec is not None:
        kw["grid_spec"] = grid_spec
    return pl.pallas_call(kernel, out_shape=out_shape, compiler_params=params, cost_estimate=cost, **kw)


def to_chunks(rows):
    width = rows.shape[-1]
    half = rows.shape[0] // 2
    low = rows[:half].reshape(-1, PT, width)
    high = rows[half:].reshape(-1, PT, width)
    return jnp.concatenate([low, high], axis=1).astype(BF)


def one_hot(feat, among):
    places = lax.broadcasted_iota(jnp.int32, (among, W), 0)
    return jnp.where(places == feat, 1.0, 0.0).astype(BF)


def pick_kernel(x_ref, go_hbm, n_hbm, out_hbm, rows_s, out_s, sems, out_sems):
    part = NT * PT // STEPS
    first = lax.rem(x_ref[0], 2) * (D // 2)
    fetches = [
        [
            pltpu.make_async_copy(
                hbm.at[f, pl.ds(i * part, part), pl.ds(pl.multiple_of(first, LANES), D // 2)],
                rows_s.at[at, i, f],
                sems.at[(at * STEPS + i) * FR + f],
            )
            for at, hbm in enumerate((go_hbm, n_hbm))
            for f in range(FR)
        ]
        for i in range(STEPS)
    ]
    for group in fetches:
        for fetch in group:
            fetch.start()
    at = lax.broadcasted_iota(jnp.int32, (1, W), 1)
    low = (at >= W // 2).astype(jnp.int32)
    z = sum((at - low * (W // 2) >= 20 * k).astype(jnp.int32) for k in range(1, 8))
    start = z * 80 + low * 40 + lax.div(x_ref[0], 2) * 20
    pick = one_hot(start + at - low * (W // 2) - z * 20, D // 2)
    chunks = NT // STEPS
    stores = []
    for i in range(STEPS):
        for fetch in fetches[i]:
            fetch.wait()
        for at in range(2):
            rows = dot(rows_s[at, i].reshape(FR * part, D // 2), pick)
            out_s[i * chunks : (i + 1) * chunks, :, at * W : (at + 1) * W] = to_chunks(rows)
        own = pl.ds(i * chunks, chunks)
        stores.append(pltpu.make_async_copy(out_s.at[own], out_hbm.at[own], out_sems.at[i]))
        stores[-1].start()
    for store in stores:
        store.wait()


def pick(x, grad_output, normed):
    hbm = pl.BlockSpec(memory_space=pl.ANY)
    shape = (NT, 2 * PT, 2 * W)
    return call(
        pick_kernel,
        jax.ShapeDtypeStruct(shape, BF),
        850_000_000,
        limit=60 * 1024 * 1024,
        in_specs=[
            pl.BlockSpec(memory_space=pltpu.SMEM),
            hbm,
            hbm,
        ],
        out_specs=hbm,
        scratch_shapes=[
            pltpu.VMEM((2, STEPS, FR, NT * PT // STEPS, D // 2), BF),
            pltpu.VMEM(shape, BF),
            pltpu.SemaphoreType.DMA((2 * STEPS * FR,)),
            pltpu.SemaphoreType.DMA((STEPS,)),
        ],
    )(x, grad_output, normed)


def pack_kernel(q_ref, k_ref, v_ref, out_ref):
    packed = [
        ref[...].reshape(FR * W, NT * PT).astype(F32).T.reshape(NT, PT, FR * W) for ref in (q_ref, k_ref, v_ref)
    ]
    out_ref[...] = jnp.concatenate(packed, axis=1).astype(BF)


def reorder_kernel(feat_ref, w_ref, out_ref):
    for at in range(NX):
        out_ref[at] = dot(w_ref[...], one_hot(feat_ref[at], D)).astype(BF)


def place(p, f):
    return (p // 4) * BLOCK + f * (BLOCK // 2) + (p % 4) * NT


def attend_kernel(x_ref, qkv_ref, gon_ref, wout_ref, wqkv_hbm, grads_ref, *rest):
    norm_refs, (wide_s, rows_s, v_s, qkvg_t, g_t, norm_s, go_s, wqkv_s, sems) = rest[:NX], rest[NX:]
    copies = [
        pltpu.make_async_copy(gon_ref.at[at, :, :, pl.ds(0, GO)], go_s.at[at], sems.at[at]) for at in range(NX)
    ]
    copies.append(pltpu.make_async_copy(wqkv_hbm, wqkv_s, sems.at[NX]))
    for copy in copies:
        copy.start()
    half = BLOCK // 2
    values = qkv_ref[...].astype(F32)
    for a in range(3):
        own = values[:, a * PT : (a + 1) * PT, :].reshape(NT * PT, FR * W)
        for t in range(HALF_TILES):
            wide_s[t, : NT * PT, :] = own[:, t * LANES : (t + 1) * LANES]
        for p in range(PT):
            for t in range(HALF_TILES):
                rows_s[p * NT : (p + 1) * NT, t * LANES : (t + 1) * LANES] = wide_s[t, pl.ds(p, NT, stride=PT), :]
        rows = rows_s[...]
        if a > 0:
            v_s[a - 1] = rows.astype(BF)
        turned = rows.T.astype(BF)
        for b in range(TOK // BLOCK):
            for f in range(FR):
                start = b * BLOCK + f * half
                qkvg_t[a * W : (a + 1) * W, start : start + half] = turned[
                    f * W : (f + 1) * W, b * half : (b + 1) * half
                ]
    acc = jnp.zeros((TOK, W), F32)
    for at in range(NX):
        copies[at].wait()
        acc = acc + dot_nt(go_s[at].reshape(TOK, GO)[:, :W], wout_ref[at])
    wide_s[0] = acc[:, :LANES]
    wide_s[1] = acc[:, LANES : 2 * LANES]
    wide_s[2, :, : W - 2 * LANES] = acc[:, 2 * LANES :]
    for p in range(PT):
        for f in range(FR):
            at = place(p, f)
            for t in range(3):
                wide = min(LANES, W - t * LANES)
                piece = wide_s[t, pl.ds(f * PT + p, NT, stride=FR * PT), :]
                g_t[at : at + NT, t * LANES : t * LANES + wide] = piece[:, :wide]
    qkvg_t[3 * W :, :] = g_t[:TOK, :W].T.astype(BF)
    row_patch = lax.broadcasted_iota(jnp.int32, (BLOCK, BLOCK), 0) // NT % 4
    col_patch = lax.broadcasted_iota(jnp.int32, (BLOCK, BLOCK), 1) // NT % 4
    same = row_patch == col_patch
    for b in range(TOK // BLOCK):
        cols = slice(b * BLOCK, (b + 1) * BLOCK)
        own = slice(b * half, (b + 1) * half)
        for h in range(HEADS):
            heads = [slice(i * W + h * HS, i * W + (h + 1) * HS) for i in range(4)]
            q_t, k_t, v_t, ga_t = [qkvg_t[head, cols] for head in heads]
            k_rows, v_rows = [
                jnp.concatenate([v_s[i, own, heads[f]] for f in range(FR)], axis=0) for i in range(2)
            ]
            scores = dot(k_rows, q_t) * TEMPER
            scores = jnp.where(same, scores, -jnp.inf)
            powers = jnp.exp(scores - jnp.max(scores, axis=0, keepdims=True))
            probs = powers * (1.0 / jnp.sum(powers, axis=0, keepdims=True))
            weights = probs.astype(BF)
            g_t[heads[3], cols] = dot(v_t, weights)
            grad_probs = dot(v_rows, ga_t)
            delta = jnp.sum(probs * grad_probs, axis=0, keepdims=True)
            grad_scores = (probs * (grad_probs - delta)).astype(BF)
            g_t[heads[0], cols] = dot(k_t, grad_scores) * TEMPER
            g_t[heads[1], cols] = dot_nt(q_t, grad_scores) * TEMPER
            g_t[heads[2], cols] = dot_nt(ga_t, weights)
    for t in range(TILES):
        tile = g_t[t * LANES : (t + 1) * LANES, :].T
        for p in range(PT):
            for f in range(FR):
                at = place(p, f)
                wide_s[t, pl.ds(f * PT + p, NT, stride=FR * PT), :] = tile[at : at + NT]
    for t in range(TILES):
        grads_ref[:, t * LANES : (t + 1) * LANES] = wide_s[t].astype(BF)
    copies[NX].wait()
    norm = dot(grads_ref[:, : 3 * W], wqkv_s[...])
    for at in range(NX):
        part = norm[:, at * W : (at + 1) * W].reshape(NT, 2 * PT, W)
        slot = lax.rem(at + NX - x_ref[0], NX)
        for f in range(FR):
            norm_s[slot, :, f * W : (f + 1) * W] = part[:, f * PT : (f + 1) * PT, :].reshape(NT * PT, W).astype(BF)
    for at in range(NX):
        norm_refs[at][...] = norm_s[at]


def attend(x, qkv, gon, w_ordered, w_qkv):
    scalar = pl.BlockSpec(memory_space=pltpu.SMEM)
    whole = pl.BlockSpec(memory_space=pltpu.VMEM)
    hbm = pl.BlockSpec(memory_space=pl.ANY)
    return call(
        attend_kernel,
        (jax.ShapeDtypeStruct((TOK, 4 * W), BF),) + (jax.ShapeDtypeStruct((TOK // 2, 2 * W), BF),) * NX,
        5_000_000_000,
        in_specs=[scalar, whole, hbm, whole, hbm],
        scratch_shapes=[
            pltpu.VMEM((TILES, TOK, LANES), F32),
            pltpu.VMEM((NT * PT, FR * W), F32),
            pltpu.VMEM((2, NT * PT, FR * W), BF),
            pltpu.VMEM((4 * W, TOK), BF),
            pltpu.VMEM((4 * W, TOK), F32),
            pltpu.VMEM((NX, TOK // 2, 2 * W), BF),
            pltpu.VMEM((NX, NT, 2 * PT, GO), BF),
            pltpu.VMEM((3 * W, D), BF),
            pltpu.SemaphoreType.DMA((NX + 1,)),
        ],
    )(x, qkv, gon, w_ordered, w_qkv)


def weight_kernel(half_ref, gon_ref, grads_ref, *refs):
    del half_ref
    out_ref = refs[-1]
    gon_t = gon_ref[0].reshape(TOK, 2 * W).T
    for rows, cols in ((slice(W, 2 * W), slice(0, 3 * W)), (slice(0, W), slice(3 * W, 4 * W))):
        total = dot(gon_t[rows], grads_ref[:, cols])
        if len(refs) == 2:
            total = total + refs[0][:, cols].astype(F32)
        out_ref[:, cols] = total.astype(BF)


def weight_half(half, gon, grads, *got):
    block = pl.BlockSpec((W, 4 * W), lambda j, half: (j, 0))
    spec = pltpu.PrefetchScalarGridSpec(
        num_scalar_prefetch=1,
        grid=(2,),
        in_specs=[
            pl.BlockSpec((1, NT, 2 * PT, 2 * W), lambda j, half: (half[0] * 2 + j, 0, 0, 0)),
            pl.BlockSpec((TOK, 4 * W), lambda j, half: (0, 0)),
        ]
        + [block] * len(got),
        out_specs=block,
    )
    shape = jax.ShapeDtypeStruct((2 * W, 4 * W), BF)
    return call(weight_kernel, shape, 4_000_000_000, spec, 20 * 1024 * 1024)(half, gon, grads, *got)


def add_kernel(*refs):
    total = refs[0][...].astype(F32)
    for ref in refs[1:-1]:
        total = total + ref[...].astype(F32)
    refs[-1][...] = total.astype(BF)


def spread_kernel(x_ref, *refs):
    out_ref = refs[-1]
    for at in range(NX):
        for k in range(NX):

            @pl.when(lax.rem(x_ref[0] + NX - k, NX) == at)
            def _(at=at, k=k):
                for f in range(FR):
                    out_ref[f, :, at * W : (at + 1) * W] = refs[k][:, f * W : (f + 1) * W]


def regroup_kernel(in_ref, out_ref):
    rows = in_ref[...].astype(F32)
    for at in range(8):
        out_ref[at] = rows[at * 20 : (at + 1) * 20].astype(BF)


def total_kernel(in_ref, qkv_ref, out_ref):
    total = in_ref[0].astype(F32)
    for at in range(1, 8):
        total = total + in_ref[at].astype(F32)
    for i in range(3):
        qkv_ref[i] = total[:, i * W : (i + 1) * W]
    out_ref[...] = total[:, 3 * W :]


def shift(array, k):
    return lax.ppermute(array, "x", [(i, (i + k) % NX) for i in range(NX)])


def on_device(queries, key_vectors, value_vectors, normed, grad_output, w_qkv, w_out):
    order = jnp.asarray(feature_order())
    x = lax.axis_index("x")
    core = lax.axis_index("core")
    scalar = pl.BlockSpec(memory_space=pltpu.SMEM)
    whole = pl.BlockSpec(memory_space=pltpu.VMEM)
    gon = pick(x.reshape(1), grad_output[0], normed[0])
    gon = lax.all_to_all(gon, TM, 0, 0, tiled=True)
    gon = lax.all_gather(gon.reshape(TOK, 2 * W), "x", axis=0, tiled=True).reshape(NX, NT, 2 * PT, 2 * W)
    qkv = call(pack_kernel, jax.ShapeDtypeStruct((NT, 3 * PT, FR * W), BF), 30_000_000_000)(
        *[jnp.swapaxes(item[0], 1, 2) for item in (queries, key_vectors, value_vectors)]
    )
    qkv = lax.all_to_all(qkv, TM, 0, 0, tiled=True)
    w_ordered = call(reorder_kernel, jax.ShapeDtypeStruct((NX, W, W), BF), 1_000_000_000)(order, w_out)
    grads, *parts = attend(x.reshape(1), qkv, gon, w_ordered, jnp.swapaxes(w_qkv, 1, 2).reshape(3 * W, D))

    moved = [parts[0]] + [shift(parts[k], k) for k in range(1, NX)]
    sent = weight_half((1 - core).reshape(1), gon, grads)
    got = lax.ppermute(sent, "core", [(0, 1), (1, 0)])
    both = weight_half(core.reshape(1), gon, grads, got).reshape(4, D // 8, 4 * W)
    quarter = lax.psum_scatter(both, Y, scatter_dimension=0, tiled=True)

    own_norm = call(add_kernel, jax.ShapeDtypeStruct((TOK // 2, 2 * W), BF), 40_000_000_000)(*moved)
    own_norm = lax.all_to_all(own_norm.reshape(NT, PT, 2 * W), TM, 0, 0, tiled=True).reshape(TOK // 2, 2 * W)
    all_norm = [own_norm] + [shift(own_norm, k) for k in range(1, NX)]
    grad_normed = call(
        spread_kernel,
        jax.ShapeDtypeStruct((FR, TOK // 2, D), BF),
        40_000_000_000,
        in_specs=[scalar] + [whole] * NX,
    )(x.reshape(1), *all_norm)

    pieces = call(regroup_kernel, jax.ShapeDtypeStruct((8, 20, 4 * W), BF), limit=60 * 1024 * 1024)(quarter.reshape(D // 8, 4 * W))
    pieces = lax.all_to_all(pieces, "z", 0, 0, tiled=True)
    grad_qkv, grad_out = call(
        total_kernel, (jax.ShapeDtypeStruct((3, 20, W), F32), jax.ShapeDtypeStruct((20, W), F32))
    )(pieces)
    return (grad_normed[None], grad_qkv, grad_out.T)


def solution(mesh):
    own = Mesh(mesh.devices.reshape(2, 8, 2, 2, 4), ("dp", "z", "yl", "core", "x"))
    in_specs = (
        P("dp", TM, None, "x"),
        P("dp", TM, None, "x"),
        P("dp", TM, None, "x"),
        P("dp", TM, None, None),
        P("dp", TM, None, None),
        P(None, None, "x"),
        P("x", None),
    )
    out_specs = (
        P("dp", TM, None, None),
        P(None, ("dp",) + TM, "x"),
        P("x", ("dp",) + TM),
    )
    return jax.shard_map(on_device, mesh=own, in_specs=in_specs, out_specs=out_specs, check_vma=False)
```
